256 devices in a mesh: level: 8 (over y, core), grp: 32 (over z, x).
Axes of the slice: x: 4, y: 4, z: 8, core: 2. Of those that a mesh axis runs over, the one named last changes fastest.
Arguments:
- right_side: bfloat16 [8, 1024, 128, 256], P('level', 'grp'), may hold values from -6 to 6
- diag_inverse: bfloat16 [8, 1024, 128, 128], P('level', 'grp'), as said below
- below_block: bfloat16 [8, 1024, 64, 128], P('level', 'grp'), may hold values from -0.75 to 0.75
- parent_device: int32 [8, 1024, 1], replicated, may hold values from 0 to 31; in each aligned block of 32 rows (0 to 31, 32 to 63, ..., all dimensions but the last counted through in order) at most 2 rows name the same one
- parent_slot: int32 [8, 1024], replicated, may hold values from 0 to 31
- row_index: int32 [8, 64, 1024], replicated, may hold values from 0 to 127, as said below
Outputs:
- solution: bfloat16 [8, 1024, 128, 256], P('level', 'grp')
- outgoing: bfloat16 [8, 1024, 64, 256], P('level', 'grp')
The draws below stay inside these ranges and needn't reach their ends.
Inputs may be any that keep to these rules, and one draw needn't show every extreme that they name: `parent_device`: among the 32 supernodes of one device, at most 2 have parents on one device; exactly 2 do on some devices. `row_index`: for each supernode, its 64 rows are distinct and increasing. `diag_inverse`: lower triangular with a positive diagonal.
All inputs are finite; a program needn't handle non-finite values.
Results may differ from the reference program's by a relative error of at most 0.009.
Values may be sent and summed in bfloat16 or wider, within the bound.
No kernel may reach another device: no remote copies, remote signals or barrier semaphores. Data moves between devices by JAX's collectives and lax.ppermute only.
A program may use at most 128 MiB of HBM per device.

```python
import math
import jax
import jax.numpy as jnp
import numpy as np
from jax import lax

S = 128
R = 64
SN_DEV = 32
CAP = 2
COLS = 256
NODES = 1024
N_LEVEL = 8
N_GRP = 32


def draw_diag_inverse(key, part):
    first, second = jax.random.split(key)
    shape = (N_LEVEL, NODES, S, S)
    rows = jax.lax.broadcasted_iota(jnp.int32, (S, S), 0)
    columns = jax.lax.broadcasted_iota(jnp.int32, (S, S), 1)
    lower = (rows > columns).astype(jnp.float32)
    eye = (rows == columns).astype(jnp.float32)
    spread = jax.random.normal(first, shape, jnp.float32) * (0.6 / jnp.sqrt(jnp.float32(S)))
    diagonal = jax.random.uniform(second, shape[:-1], jnp.float32, 0.6, 1.1)
    return (lower * spread + eye * diagonal[..., None]).astype(jnp.bfloat16)


def draw_row_index(key, part):
    keys = jax.random.split(key, N_LEVEL * NODES)
    chosen = jax.vmap(lambda single: jax.random.permutation(single, S)[:R])(keys)
    chosen = jnp.sort(chosen, axis=1).astype(jnp.int32).reshape(N_LEVEL, NODES, R)
    return jnp.transpose(chosen, (0, 2, 1))


def with_ends(array, key, low, largest):
    index_at = [jax.random.randint(jax.random.fold_in(key, axis), (), 0, length) for axis, length in enumerate(array.shape)]
    longest = array.shape.index(max(array.shape))
    next_to = index_at[:longest] + [(index_at[longest] + 1) % array.shape[longest]] + index_at[longest + 1:]
    return array.at[tuple(index_at)].set(low).at[tuple(next_to)].set(largest)


def block_scale(own_key, shape, pieces, smallest, high):
    gain = 1.0
    for axis_at, blocks in pieces:
        draws = jax.random.uniform(jax.random.fold_in(jax.random.fold_in(own_key, 6), axis_at), (blocks,), jnp.float32, smallest / len(pieces), high / len(pieces))
        gain = gain * jnp.repeat(jnp.exp(draws), shape[axis_at] // blocks).reshape((-1,) + (1,) * (len(shape) - 1 - axis_at))
    return gain


def assign_block(key, own, number, rows, amount, top, most, lean):
    ranking = jax.random.permutation(key, amount)
    packed, common = load_shares(amount, rows * top, most, lean, True), load_shares(amount, rows * top, most, lean, False)
    places = jnp.arange(amount)

    def named(lengths, turn):
        used = int((lengths > 0).sum())
        fixed = max(1, used // 4)
        moved = fixed + (places - fixed + turn * (used - fixed)) % max(1, amount - fixed)
        return jnp.zeros((amount,), jnp.int32).at[ranking[jnp.where(places < fixed, places, moved)]].set(jnp.asarray(lengths, jnp.int32))

    lengths = jnp.where(number % 4 == 0, named(packed, number // 4), named(common, number - number // 4 - 1))
    mixed = jax.random.permutation(jax.random.fold_in(own, 3), amount)
    source_of, taker = mixed[0:amount // 2 * 2:2], mixed[1:amount // 2 * 2:2]
    slack = jnp.minimum(lengths[source_of] - 1, most - lengths[taker]) // 2
    slack = jnp.where((source_of == ranking[0]) | (taker == ranking[0]) | (lengths[taker] == 0), 0, jnp.maximum(slack, 0))
    moved = jax.random.randint(jax.random.fold_in(own, 4), (amount // 2,), 0, 1 << 20) % (slack + 1)
    lengths = lengths.at[source_of].add(-moved).at[taker].add(moved)
    items = jnp.searchsorted(jnp.cumsum(lengths), jnp.arange(rows * top), side="right").astype(jnp.int32)
    listing = items.reshape(top, rows).T
    listing = listing[jax.random.permutation(jax.random.fold_in(own, 1), rows)]
    turn = jax.random.randint(jax.random.fold_in(own, 2), (rows, 1), 0, top)
    return jnp.take_along_axis(listing, (jnp.arange(top)[None, :] + turn) % top, axis=1)


def load_shares(number_of, total, reach, skew, full):
    weights = [(1 << 20) // math.isqrt(standing ** skew) + 1 for standing in range(1, number_of + 1)]
    largest = reach if full else min(reach, max(-(-total // number_of), total * weights[0] // sum(weights)))
    least = 1 if total - largest >= number_of - 1 else 0
    given, spare = [largest] + [least] * (number_of - 1), total - largest - least * (number_of - 1)
    while spare > 0:
        free = [i for i in range(1, number_of) if given[i] < largest] or [i for i in range(1, number_of) if given[i] < reach]
        mass, budget = sum([weights[i] for i in free]), spare
        for i in free:
            more = min(reach - given[i], max(1, budget * weights[i] // mass), spare)
            given[i] = given[i] + more
            spare = spare - more
    return np.array(given)


def scatter_about(rng, extent, scale, most, cuts=(), held_as=jnp.bfloat16):
    result = jax.random.normal(rng, extent, jnp.float32) * scale
    if len(cuts) > 0:
        result = block_scale(rng, extent, cuts, -0.22, 0.18) * result
    return jnp.clip(result, min=-most, max=most).astype(held_as)


def setup_inputs(seed: int = 0) -> dict:
    arg_keys = jax.random.split(jax.random.key(seed), 7)
    right_side = scatter_about(arg_keys[0], (N_LEVEL, NODES, S, COLS), 1.0, 6.0, ((0, 8), (1, 32)))
    diag_inverse = draw_diag_inverse(jax.random.fold_in(arg_keys[6], 71), 0)
    below_block = scatter_about(arg_keys[2], (N_LEVEL, NODES, R, S), (S // 2) ** -0.5, 0.75, ((0, 8), (1, 32)))
    parent_device_keys = jax.random.split(jax.random.fold_in(arg_keys[3], 1), N_LEVEL * NODES // SN_DEV)
    parent_device_turns = jax.random.permutation(jax.random.fold_in(arg_keys[3], 3), N_LEVEL * NODES // SN_DEV)
    parent_device = jax.vmap(lambda own, number: assign_block(jax.random.fold_in(arg_keys[3], 2), own, number, SN_DEV, N_GRP, 1, CAP, 2))(parent_device_keys, parent_device_turns).reshape((N_LEVEL, NODES, 1))
    parent_slot = with_ends(jax.random.randint(arg_keys[4], (N_LEVEL, NODES), 0, SN_DEV), jax.random.fold_in(arg_keys[4], 1), 0, SN_DEV - 1).astype(jnp.int32)
    row_index = draw_row_index(jax.random.fold_in(arg_keys[6], 71), 0)
    return {"right_side": right_side, "diag_inverse": diag_inverse, "below_block": below_block, "parent_device": parent_device, "parent_slot": parent_slot, "row_index": row_index}


def widen(value):
    return lax.optimization_barrier(value).astype(jnp.float32)


def reference(right_side, diag_inverse, below_block, parent_device, parent_slot, row_index):
    inflow = jnp.zeros((NODES, S, COLS), jnp.float32)
    solved_all = []
    updates_all = []
    for level in range(N_LEVEL):
        reduced = (right_side[level].astype(jnp.float32) - inflow).astype(jnp.bfloat16)
        solved = jnp.einsum("nij,njc->nic", diag_inverse[level].astype(jnp.float32), widen(reduced)).astype(jnp.bfloat16)
        update = jnp.einsum("nri,nic->nrc", below_block[level].astype(jnp.float32), widen(solved)).astype(jnp.bfloat16)
        solved_all.append(solved)
        updates_all.append(update)
        target = (parent_device[level, :, 0] * SN_DEV + parent_slot[level]).astype(jnp.int32)
        placed = (target[:, None] * S + jnp.transpose(row_index[level])).astype(jnp.int32)
        inflow = jnp.zeros((NODES * S, COLS), jnp.float32).at[placed.reshape(-1)].add(
            update.astype(jnp.float32).reshape(-1, COLS)).reshape(NODES, S, COLS)
    return jnp.stack(solved_all), jnp.stack(updates_all)
```

```python
import functools

import jax
import jax.numpy as jnp
from jax import lax
from jax.experimental import pallas as pl
from jax.experimental.pallas import tpu as pltpu
from jax.sharding import PartitionSpec as P

VMEM = 48 * 1024 * 1024
F32 = jnp.float32
BF16 = jnp.bfloat16


def dot(a, b):
    return jnp.dot(a, b, preferred_element_type=F32)


def dot_nt(a, b):
    return lax.dot_general(a, b, (((1,), (1,)), ((), ())), preferred_element_type=F32)


def low_lanes(shape, half):
    return lax.broadcasted_iota(jnp.int32, shape, len(shape) - 1) < half


def prepare_kernel(rhs_ref, inv_ref, below_ref, gain_ref, load_ref):
    nodes = rhs_ref.shape[0]
    levels, _, span, _ = load_ref.shape
    for pair in range(nodes // 2):
        halves = []
        for node in (2 * pair, 2 * pair + 1):
            inv, below = inv_ref[node], below_ref[node]
            gain_ref[node] = dot(below, inv).astype(BF16)
            solved = dot(inv, rhs_ref[node]).astype(BF16)
            halves.append(dot(below, solved))
        both = jnp.concatenate(halves, axis=0).T.astype(BF16)
        load_ref[:, pair] = both.reshape(levels, span, both.shape[1])


def operator_kernel(slot_ref, rows_ref, gain_ref, op_ref):
    senders, rows, lanes = op_ref.shape
    nodes, _, block = gain_ref.shape
    low = low_lanes((rows, lanes), rows)
    for s in range(senders):
        hot = (
            lax.broadcasted_iota(jnp.int32, (block, lanes), 0) == rows_ref[s : s + 1, :]
        ).astype(BF16)
        first = dot(gain_ref[jnp.minimum(slot_ref[2 * s], nodes - 1)], hot)
        second = dot(gain_ref[jnp.minimum(slot_ref[2 * s + 1], nodes - 1)], hot)
        op_ref[s] = jnp.where(low, first, second).astype(BF16)


def pack(values, take_ref, level, send_ref):
    senders, span, lanes = send_ref.shape
    low = low_lanes((span, lanes), lanes // 2)
    for d in range(senders):
        first = values[take_ref[level, 2 * d]]
        second = values[take_ref[level, 2 * d + 1]]
        send_ref[d] = jnp.where(low, first, second)


def both_halves(pair_value, odd, low, half):
    turned = pltpu.roll(pair_value, half, 1)
    return jnp.where(low, turned, pair_value) if odd else jnp.where(low, pair_value, turned)


def first_kernel(take_ref, load_ref, send_ref, values):
    _, pairs, span, lanes = load_ref.shape
    low = low_lanes((span, lanes), lanes // 2)
    for pair in range(pairs):
        value = load_ref[0, pair].astype(F32)
        for odd in (0, 1):
            values[2 * pair + odd] = both_halves(value, odd, low, lanes // 2).astype(BF16)
    values[2 * pairs] = jnp.zeros((span, lanes), BF16)
    pack(values, take_ref, 0, send_ref)


def hop_kernel(level, take_ref, slot_ref, got_ref, op_ref, load_ref, send_ref, total, values):
    senders, span, lanes = got_ref.shape
    _, pairs, _, _ = load_ref.shape
    half = lanes // 2
    low = low_lanes((span, lanes), half)
    low_op = low_lanes((half, lanes), half)
    total[...] = jnp.zeros_like(total)
    for s in range(senders):
        op = op_ref[0, s]
        zero = jnp.zeros_like(op)
        split = jnp.concatenate(
            [jnp.where(low_op, op, zero), jnp.where(low_op, zero, op)], axis=0
        )
        part = dot_nt(got_ref[s], split)
        one = slot_ref[level - 1, 2 * s]
        two = slot_ref[level - 1, 2 * s + 1]
        total[one] += jnp.where(low, part, 0.0)
        total[two] += jnp.where(low, 0.0, part)
    for pair in range(pairs):
        value = load_ref[0, pair].astype(F32)
        for odd in (0, 1):
            node = 2 * pair + odd
            come = total[node]
            come = come + pltpu.roll(come, half, 1)
            values[node] = (both_halves(value, odd, low, half) - come).astype(BF16)
    values[2 * pairs] = jnp.zeros((span, lanes), BF16)
    pack(values, take_ref, level, send_ref)


def finish_kernel(
    steps, slot_ref, rows_ref, got_ref, rhs_ref, inv_ref, below_ref, sol_ref, out_ref, inflow
):
    step = pl.program_id(0)
    chunks, senders, span, lanes = got_ref.shape
    block = rhs_ref.shape[1]
    half = lanes // 2

    @pl.when(step == 0)
    def _():
        inflow[...] = jnp.zeros_like(inflow)

    @pl.when(step < steps)
    def _():
        low = low_lanes((block, lanes), half)
        for s in range(senders):
            rows = rows_ref[pl.ds(step * senders + s, 1), :]
            hot = lax.broadcasted_iota(jnp.int32, (block, lanes), 0) == rows
            hot = jnp.concatenate(
                [jnp.logical_and(hot, low), jnp.logical_and(hot, jnp.logical_not(low))], axis=0
            )
            got = got_ref[:, s].reshape(chunks * span, lanes)
            part = dot_nt(hot.astype(BF16), got)
            one = slot_ref[2 * (step * senders + s)]
            two = slot_ref[2 * (step * senders + s) + 1]
            inflow[one] += part[:block]
            inflow[two] += part[block:]

    @pl.when(step >= steps)
    def _():
        nodes = rhs_ref.shape[0]
        base = (step - steps) * nodes
        for n in range(nodes):
            reduced = (rhs_ref[n].astype(F32) - inflow[base + n]).astype(BF16)
            solved = dot(inv_ref[n], reduced).astype(BF16)
            sol_ref[0, n] = solved
            out_ref[0, n] = dot(below_ref[n], solved).astype(BF16)


def params(*semantics):
    return pltpu.CompilerParams(vmem_limit_bytes=VMEM, dimension_semantics=semantics or None)


SMEM_SPEC = pl.BlockSpec(memory_space=pltpu.SMEM)
VMEM_SPEC = pl.BlockSpec(memory_space=pltpu.VMEM)


def shards(right_side, diag_inverse, below_block, parent_device, parent_slot, row_index):
    levels = lax.axis_size("level")
    group = lax.axis_size("grp")
    level_id = lax.axis_index("level")
    member = lax.axis_index("grp")
    _, nodes, block, columns = right_side.shape
    rows = below_block.shape[2]
    span = columns // levels
    lanes = 2 * rows
    pairs = nodes // 2
    hops = levels - 1

    devices = parent_device[:hops, :, 0].reshape(hops, group, nodes)
    slots = parent_slot[:hops].reshape(hops, group, nodes)
    place = lax.broadcasted_iota(jnp.int32, (hops, group, nodes), 2)

    def ends(named):
        first = jnp.min(jnp.where(named, place, nodes), axis=-1)
        last = jnp.max(jnp.where(named, place, -1), axis=-1)
        return first, jnp.where(last > first, last, nodes)

    first, last = ends(devices == member)
    own = lax.dynamic_index_in_dim(devices, member, 1, keepdims=True)
    take = jnp.stack(ends(own == lax.broadcasted_iota(jnp.int32, (hops, group, nodes), 1)), -1)
    take = take.reshape(hops, 2 * group)

    def slot_of(which):
        hit = place == which[..., None]
        found = jnp.sum(jnp.where(hit, slots, 0), axis=-1)
        return jnp.where(which < nodes, found, nodes)

    slot = jnp.stack([slot_of(first), slot_of(last)], -1).reshape(hops, 2 * group)

    before = jnp.maximum(level_id - 1, 0)
    home_slot = lax.dynamic_index_in_dim(slot, before, 0, keepdims=False)
    home_slot = jnp.where(level_id > 0, home_slot, nodes)
    landing = lax.dynamic_index_in_dim(row_index, before, 0, keepdims=False)
    landing = landing.reshape(rows, group, nodes)

    def rows_of(which):
        which = lax.dynamic_index_in_dim(which, before, 0, keepdims=False)[None, :, None]
        hit = lax.broadcasted_iota(jnp.int32, (rows, group, nodes), 2) == which
        found = jnp.sum(jnp.where(hit, landing, 0), axis=-1)
        return jnp.where(which[..., 0] < nodes, found, -1)

    home_rows = jnp.concatenate([rows_of(first), rows_of(last)], axis=0).T

    step = 4
    gain, load = pl.pallas_call(
        prepare_kernel,
        grid=(nodes // step,),
        in_specs=[
            pl.BlockSpec((step, block, columns), lambda i: (i, 0, 0)),
            pl.BlockSpec((step, block, block), lambda i: (i, 0, 0)),
            pl.BlockSpec((step, rows, block), lambda i: (i, 0, 0)),
        ],
        out_specs=[
            pl.BlockSpec((step, rows, block), lambda i: (i, 0, 0)),
            pl.BlockSpec((levels, step // 2, span, lanes), lambda i: (0, i, 0, 0)),
        ],
        out_shape=[
            jax.ShapeDtypeStruct((nodes, rows, block), BF16),
            jax.ShapeDtypeStruct((levels, pairs, span, lanes), BF16),
        ],
        compiler_params=params("arbitrary"),
        name="prepare",
    )(right_side[0], diag_inverse[0], below_block[0])

    operators = pl.pallas_call(
        operator_kernel,
        in_specs=[SMEM_SPEC, VMEM_SPEC, VMEM_SPEC],
        out_specs=VMEM_SPEC,
        out_shape=jax.ShapeDtypeStruct((group, rows, lanes), BF16),
        compiler_params=params(),
        name="operators",
    )(home_slot, home_rows, gain)
    operators = lax.all_gather(operators, "level", axis=0)
    loads = lax.all_to_all(load, "level", split_axis=0, concat_axis=0, tiled=True)

    def load_spec(level):
        return pl.BlockSpec((1, pairs, span, lanes), lambda i: (level, 0, 0, 0))

    message = jax.ShapeDtypeStruct((group, span, lanes), BF16)
    message_spec = pl.BlockSpec((group, span, lanes), lambda i: (0, 0, 0))
    values_shape = pltpu.VMEM((nodes + 1, span, lanes), BF16)
    arrived = [jnp.zeros((group, span, lanes), BF16)]
    for level in range(hops):
        if level == 0:
            send = pl.pallas_call(
                first_kernel,
                grid=(1,),
                in_specs=[SMEM_SPEC, load_spec(0)],
                out_specs=message_spec,
                out_shape=message,
                scratch_shapes=[values_shape],
                compiler_params=params("arbitrary"),
                name="first",
            )(take, loads)
        else:
            send = pl.pallas_call(
                functools.partial(hop_kernel, level),
                grid=(1,),
                in_specs=[
                    SMEM_SPEC,
                    SMEM_SPEC,
                    message_spec,
                    pl.BlockSpec((1, group, rows, lanes), lambda i, level=level: (level, 0, 0, 0)),
                    load_spec(level),
                ],
                out_specs=message_spec,
                out_shape=message,
                scratch_shapes=[pltpu.VMEM((nodes + 1, span, lanes), F32), values_shape],
                compiler_params=params("arbitrary"),
                name="hop",
            )(take, slot, arrived[-1], operators, loads)
        arrived.append(lax.all_to_all(send, "grp", split_axis=0, concat_axis=0, tiled=True))

    home = lax.all_to_all(jnp.stack(arrived), "level", split_axis=0, concat_axis=0, tiled=True)

    steps = group // step
    turns = nodes // step
    lead = lambda i: jnp.minimum(i, steps - 1)
    tail = lambda i: jnp.maximum(i - steps, 0)
    return pl.pallas_call(
        functools.partial(finish_kernel, steps),
        grid=(steps + turns,),
        in_specs=[
            SMEM_SPEC,
            VMEM_SPEC,
            pl.BlockSpec((levels, step, span, lanes), lambda i: (0, lead(i), 0, 0)),
            pl.BlockSpec((step, block, columns), lambda i: (tail(i), 0, 0)),
            pl.BlockSpec((step, block, block), lambda i: (tail(i), 0, 0)),
            pl.BlockSpec((step, rows, block), lambda i: (tail(i), 0, 0)),
        ],
        out_specs=[
            pl.BlockSpec((1, step, block, columns), lambda i: (0, tail(i), 0, 0)),
            pl.BlockSpec((1, step, rows, columns), lambda i: (0, tail(i), 0, 0)),
        ],
        out_shape=[
            jax.ShapeDtypeStruct((1, nodes, block, columns), BF16),
            jax.ShapeDtypeStruct((1, nodes, rows, columns), BF16),
        ],
        scratch_shapes=[pltpu.VMEM((nodes + 1, block, columns), F32)],
        compiler_params=params("arbitrary"),
        name="finish",
    )(home_slot, home_rows, home, right_side[0], diag_inverse[0], below_block[0])


def solution(mesh):
    return jax.shard_map(
        shards,
        mesh=mesh,
        in_specs=(
            P("level", "grp", None, None),
            P("level", "grp", None, None),
            P("level", "grp", None, None),
            P(),
            P(),
            P(),
        ),
        out_specs=(P("level", "grp", None, None), P("level", "grp", None, None)),
        check_vma=False,
    )
```

```python
import functools

import jax
import jax.numpy as jnp
from jax import lax
from jax.experimental import pallas as pl
from jax.experimental.pallas import tpu as pltpu
from jax.sharding import PartitionSpec as P

F32 = jnp.float32
BF16 = jnp.bfloat16


def dot(a, b):
    return jnp.dot(a, b, preferred_element_type=F32)


def dot_nt(a, b):
    return lax.dot_general(a, b, (((1,), (1,)), ((), ())), preferred_element_type=F32)


def low_lanes(shape, half):
    return lax.broadcasted_iota(jnp.int32, shape, len(shape) - 1) < half


def prepare_kernel(rhs_ref, inv_ref, below_ref, gain_ref, load_ref):
    nodes = rhs_ref.shape[0]
    levels, _, span, _ = load_ref.shape
    for pair in range(nodes // 2):
        halves = []
        for node in (2 * pair, 2 * pair + 1):
            inv, below = inv_ref[node], below_ref[node]
            gain_ref[node] = dot(below, inv).astype(BF16)
            solved = dot(inv, rhs_ref[node]).astype(BF16)
            halves.append(dot(below, solved))
        both = jnp.concatenate(halves, axis=0).T.astype(BF16)
        load_ref[:, pair] = both.reshape(levels, span, both.shape[1])


def operator_kernel(slot_ref, rows_ref, gain_ref, op_ref):
    senders, rows, lanes = op_ref.shape
    nodes, _, block = gain_ref.shape
    low = low_lanes((rows, lanes), rows)
    for s in range(senders):
        hot = (
            lax.broadcasted_iota(jnp.int32, (block, lanes), 0) == rows_ref[s : s + 1, :]
        ).astype(BF16)
        first = dot(gain_ref[jnp.minimum(slot_ref[2 * s], nodes - 1)], hot)
        second = dot(gain_ref[jnp.minimum(slot_ref[2 * s + 1], nodes - 1)], hot)
        op_ref[s] = jnp.where(low, first, second).astype(BF16)


def pack(values, take_ref, level, send_ref):
    senders, span, lanes = send_ref.shape
    low = low_lanes((span, lanes), lanes // 2)
    for d in range(senders):
        first = values[take_ref[level, 2 * d]]
        second = values[take_ref[level, 2 * d + 1]]
        send_ref[d] = jnp.where(low, first, second)


def both_halves(pair_value, odd, low, half):
    turned = pltpu.roll(pair_value, half, 1)
    return jnp.where(low, turned, pair_value) if odd else jnp.where(low, pair_value, turned)


def first_kernel(take_ref, load_ref, send_ref, values):
    _, pairs, span, lanes = load_ref.shape
    low = low_lanes((span, lanes), lanes // 2)
    for pair in range(pairs):
        value = load_ref[0, pair].astype(F32)
        for odd in (0, 1):
            values[2 * pair + odd] = both_halves(value, odd, low, lanes // 2).astype(BF16)
    values[2 * pairs] = jnp.zeros((span, lanes), BF16)
    pack(values, take_ref, 0, send_ref)


def hop_kernel(
    level,
    take_ref,
    slot_ref,
    got_ref,
    op_ref,
    load_ref,
    send_ref,
    got,
    ops,
    load,
    total,
    values,
    ready,
):
    senders, span, lanes = got.shape
    pairs = load.shape[0]
    half = lanes // 2
    parts = ready.shape[1]
    share = senders // parts
    copies = []
    for i in range(parts):
        where = pl.ds(i * share, share)
        copies.append(
            (
                pltpu.make_async_copy(got_ref.at[where], got.at[where], ready.at[0, i]),
                pltpu.make_async_copy(op_ref.at[level, where], ops.at[where], ready.at[1, i]),
            )
        )
    loading = pltpu.make_async_copy(load_ref.at[level], load, ready.at[2, 0])
    for pair in copies:
        for copy in pair:
            copy.start()
    loading.start()
    low = low_lanes((span, lanes), half)
    low_op = low_lanes((half, lanes), half)
    total[...] = jnp.zeros_like(total)
    for s in range(senders):
        if s % share == 0:
            for copy in copies[s // share]:
                copy.wait()
        op = ops[s]
        zero = jnp.zeros_like(op)
        split = jnp.concatenate(
            [jnp.where(low_op, op, zero), jnp.where(low_op, zero, op)], axis=0
        )
        part = dot_nt(got[s], split)
        one = slot_ref[level - 1, 2 * s]
        two = slot_ref[level - 1, 2 * s + 1]
        total[one] += jnp.where(low, part, 0.0)
        total[two] += jnp.where(low, 0.0, part)
    loading.wait()
    for pair in range(pairs):
        value = load[pair].astype(F32)
        for odd in (0, 1):
            node = 2 * pair + odd
            come = total[node]
            come = come + pltpu.roll(come, half, 1)
            values[node] = (both_halves(value, odd, low, half) - come).astype(BF16)
    values[2 * pairs] = jnp.zeros((span, lanes), BF16)
    pack(values, take_ref, level, send_ref)


def finish_kernel(
    early_counts,
    level_ref,
    slot_ref,
    rows_ref,
    rhs_ref,
    inv_ref,
    below_ref,
    *rest,
):
    chunks, parts = rest[-1].shape
    groups = len(early_counts)
    early = rest[:groups]
    sol_ref, out_ref, got, rhs, inv, below, inflow, base_ready, ready = rest[-9:]
    late = rest[groups:-9]
    late = [late[i : i + chunks] for i in range(0, len(late), chunks)]
    level = level_ref[0]
    step = pl.program_id(0)
    _, senders, span, lanes = got.shape
    _, nodes, block, _ = sol_ref.shape
    half = lanes // 2
    share = senders // parts
    spots = [pl.ds(p * share, share) for p in range(parts)]
    base = [
        pltpu.make_async_copy(source, target, base_ready.at[i])
        for i, (source, target) in enumerate(((rhs_ref, rhs), (inv_ref, inv), (below_ref, below)))
    ]

    @pl.when(step == 0)
    def _():
        def fetch(source):
            for p, spot in enumerate(spots):
                for c in range(chunks):
                    pltpu.make_async_copy(
                        source(c).at[spot], got.at[c, spot], ready.at[c, p]
                    ).start()

        reach = 1
        for index, (array, count) in enumerate(zip(early, early_counts)):
            inside = level < reach + count
            if index > 0:
                inside = jnp.logical_and(inside, level >= reach)

            @pl.when(inside)
            def _(array=array, reach=reach):
                fetch(lambda c: array.at[c, jnp.maximum(level - reach, 0)])

            reach += count
        for arrays in late:

            @pl.when(level == reach)
            def _(arrays=arrays):
                fetch(lambda c: arrays[c])

            reach += 1
        for copy in base:
            copy.start()

        inflow[...] = jnp.zeros_like(inflow)
        low = low_lanes((block, lanes), half)
        for s in range(senders):
            if s % share == 0:
                p = s // share
                for c in range(chunks):
                    pltpu.make_async_copy(
                        got.at[c, spots[p]], got.at[c, spots[p]], ready.at[c, p]
                    ).wait()
            hot = lax.broadcasted_iota(jnp.int32, (block, lanes), 0) == rows_ref[s : s + 1, :]
            hot = jnp.concatenate(
                [jnp.logical_and(hot, low), jnp.logical_and(hot, jnp.logical_not(low))], axis=0
            )
            part = dot(hot.astype(BF16), got[:, s].reshape(chunks * span, lanes).T)
            inflow[slot_ref[2 * s]] += part[:block]
            inflow[slot_ref[2 * s + 1]] += part[block:]
        for copy in base:
            copy.wait()

    @pl.when(step > 0)
    def _():
        at = (step - 1) * nodes
        reduced = [
            (rhs[at + n].astype(F32) - inflow[at + n]).astype(BF16) for n in range(nodes)
        ]
        solved = [dot(inv[at + n], reduced[n]).astype(BF16) for n in range(nodes)]
        for n in range(nodes):
            sol_ref[0, n] = solved[n]
        for n in range(nodes):
            out_ref[0, n] = dot(below[at + n], solved[n]).astype(BF16)


def params(limit, *semantics):
    return pltpu.CompilerParams(
        vmem_limit_bytes=limit * 1024 * 1024, dimension_semantics=semantics or None
    )


SMEM_SPEC = pl.BlockSpec(memory_space=pltpu.SMEM)
VMEM_SPEC = pl.BlockSpec(memory_space=pltpu.VMEM)
HBM_SPEC = pl.BlockSpec(memory_space=pltpu.HBM)


def shards(right_side, diag_inverse, below_block, parent_device, parent_slot, row_index):
    levels = lax.axis_size("level")
    group = lax.axis_size("grp")
    level_id = lax.axis_index("level")
    member = lax.axis_index("grp")
    _, nodes, block, columns = right_side.shape
    rows = below_block.shape[2]
    span = columns // levels
    lanes = 2 * rows
    pairs = nodes // 2
    hops = levels - 1

    step = 4
    gain, load = pl.pallas_call(
        prepare_kernel,
        grid=(nodes // step,),
        in_specs=[
            pl.BlockSpec((step, block, columns), lambda i: (i, 0, 0)),
            pl.BlockSpec((step, block, block), lambda i: (i, 0, 0)),
            pl.BlockSpec((step, rows, block), lambda i: (i, 0, 0)),
        ],
        out_specs=[
            pl.BlockSpec((step, rows, block), lambda i: (i, 0, 0)),
            pl.BlockSpec((levels, step // 2, span, lanes), lambda i: (0, i, 0, 0)),
        ],
        out_shape=[
            jax.ShapeDtypeStruct((nodes, rows, block), BF16),
            jax.ShapeDtypeStruct((levels, pairs, span, lanes), BF16),
        ],
        compiler_params=params(60, "arbitrary"),
        name="prepare",
    )(right_side[0], diag_inverse[0], below_block[0])

    devices = parent_device[:hops, :, 0].reshape(hops, group, nodes)
    slots = parent_slot[:hops].reshape(hops, group, nodes)
    place = lax.broadcasted_iota(jnp.int32, (hops, group, nodes), 2)

    def ends(named):
        first = jnp.min(jnp.where(named, place, nodes), axis=-1)
        last = jnp.max(jnp.where(named, place, -1), axis=-1)
        return first, jnp.where(last > first, last, nodes)

    first, last = ends(devices == member)
    own = lax.dynamic_index_in_dim(devices, member, 1, keepdims=True)
    take = jnp.stack(ends(own == lax.broadcasted_iota(jnp.int32, (hops, group, nodes), 1)), -1)
    take = take.reshape(hops, 2 * group)

    def slot_of(which):
        hit = place == which[..., None]
        found = jnp.sum(jnp.where(hit, slots, 0), axis=-1)
        return jnp.where(which < nodes, found, nodes)

    slot = jnp.stack([slot_of(first), slot_of(last)], -1).reshape(hops, 2 * group)

    before = jnp.maximum(level_id - 1, 0)
    home_slot = lax.dynamic_index_in_dim(slot, before, 0, keepdims=False)
    home_slot = jnp.where(level_id > 0, home_slot, nodes)
    landing = lax.dynamic_index_in_dim(row_index, before, 0, keepdims=False)
    landing = landing.reshape(rows, group, nodes)

    def rows_of(which):
        which = lax.dynamic_index_in_dim(which, before, 0, keepdims=False)[None, :, None]
        hit = lax.broadcasted_iota(jnp.int32, (rows, group, nodes), 2) == which
        found = jnp.sum(jnp.where(hit, landing, 0), axis=-1)
        return jnp.where(which[..., 0] < nodes, found, -1)

    home_rows = jnp.concatenate([rows_of(first), rows_of(last)], axis=0).T

    operators = pl.pallas_call(
        operator_kernel,
        in_specs=[SMEM_SPEC, VMEM_SPEC, VMEM_SPEC],
        out_specs=VMEM_SPEC,
        out_shape=jax.ShapeDtypeStruct((group, rows, lanes), BF16),
        compiler_params=params(16),
        name="operators",
    )(home_slot, home_rows, gain)
    operators = lax.all_gather(operators, "level", axis=0)
    loads = lax.all_to_all(load, "level", split_axis=0, concat_axis=0, tiled=True)

    message = jax.ShapeDtypeStruct((group, span, lanes), BF16)
    values_shape = pltpu.VMEM((nodes + 1, span, lanes), BF16)
    arrived = [None]
    early_counts = (hops // 2, hops - 2 - hops // 2)
    early = []
    for level in range(hops):
        if level == 0:
            send = pl.pallas_call(
                first_kernel,
                in_specs=[SMEM_SPEC, VMEM_SPEC],
                out_specs=VMEM_SPEC,
                out_shape=message,
                scratch_shapes=[values_shape],
                compiler_params=params(16),
                name="first",
            )(take, loads)
        else:
            send = pl.pallas_call(
                functools.partial(hop_kernel, level),
                in_specs=[SMEM_SPEC, SMEM_SPEC, HBM_SPEC, HBM_SPEC, HBM_SPEC],
                out_specs=VMEM_SPEC,
                out_shape=message,
                scratch_shapes=[
                    pltpu.VMEM((group, span, lanes), BF16),
                    pltpu.VMEM((group, rows, lanes), BF16),
                    pltpu.VMEM((pairs, span, lanes), BF16),
                    pltpu.VMEM((nodes + 1, span, lanes), F32),
                    values_shape,
                    pltpu.SemaphoreType.DMA((3, 4)),
                ],
                compiler_params=params(53),
                name="hop",
            )(take, slot, arrived[-1], operators, loads)
        arrived.append(lax.all_to_all(send, "grp", split_axis=0, concat_axis=0, tiled=True))
        if len(arrived) == 1 + sum(early_counts[: len(early) + 1]) and len(early) < 2:
            ready = jnp.stack(arrived[1 + sum(early_counts[: len(early)]) :])
            early.append(lax.all_gather(ready, "level", axis=0))
        elif len(arrived) == hops:
            arrived[-1], early[0] = lax.optimization_barrier((arrived[-1], early[0]))

    late = []
    for level in range(1 + sum(early_counts), levels):
        late += [
            arrived[level]
            if c == level
            else lax.ppermute(arrived[level], "level", [(c, level)])
            for c in range(levels)
        ]

    step = 8
    parts = 4
    tail = lambda i: jnp.maximum(i - 1, 0)
    return pl.pallas_call(
        functools.partial(finish_kernel, early_counts),
        grid=(1 + nodes // step,),
        in_specs=[SMEM_SPEC, SMEM_SPEC, VMEM_SPEC]
        + [HBM_SPEC] * (3 + len(early) + len(late)),
        out_specs=[
            pl.BlockSpec((1, step, block, columns), lambda i: (0, tail(i), 0, 0)),
            pl.BlockSpec((1, step, rows, columns), lambda i: (0, tail(i), 0, 0)),
        ],
        out_shape=[
            jax.ShapeDtypeStruct((1, nodes, block, columns), BF16),
            jax.ShapeDtypeStruct((1, nodes, rows, columns), BF16),
        ],
        scratch_shapes=[
            pltpu.VMEM((levels, group, span, lanes), BF16),
            pltpu.VMEM((nodes, block, columns), BF16),
            pltpu.VMEM((nodes, block, block), BF16),
            pltpu.VMEM((nodes, rows, block), BF16),
            pltpu.VMEM((nodes + 1, block, columns), F32),
            pltpu.SemaphoreType.DMA((3,)),
            pltpu.SemaphoreType.DMA((levels, parts)),
        ],
        compiler_params=params(50, "arbitrary"),
        name="finish",
    )(
        level_id.reshape(1),
        home_slot,
        home_rows,
        right_side[0],
        diag_inverse[0],
        below_block[0],
        *early,
        *late,
    )


def solution(mesh):
    return jax.shard_map(
        shards,
        mesh=mesh,
        in_specs=(
            P("level", "grp", None, None),
            P("level", "grp", None, None),
            P("level", "grp", None, None),
            P(),
            P(),
            P(),
        ),
        out_specs=(P("level", "grp", None, None), P("level", "grp", None, None)),
        check_vma=False,
    )
```

```python
import functools

import jax
import jax.numpy as jnp
from jax import lax
from jax.experimental import pallas as pl
from jax.experimental.pallas import tpu as pltpu
from jax.sharding import PartitionSpec as P

F32 = jnp.float32
BF16 = jnp.bfloat16


def dot(a, b):
    return jnp.dot(a, b, preferred_element_type=F32)


def dot_nt(a, b):
    return lax.dot_general(a, b, (((1,), (1,)), ((), ())), preferred_element_type=F32)


def low_lanes(shape, half):
    return lax.broadcasted_iota(jnp.int32, shape, len(shape) - 1) < half


def prepare_kernel(rhs_ref, inv_ref, below_ref, gain_ref, load_ref):
    nodes = rhs_ref.shape[0]
    levels, _, span, _ = load_ref.shape
    for pair in range(nodes // 2):
        halves = []
        for node in (2 * pair, 2 * pair + 1):
            inv, below = inv_ref[node], below_ref[node]
            gain_ref[node] = dot(below, inv).astype(BF16)
            solved = dot(inv, rhs_ref[node]).astype(BF16)
            halves.append(dot(below, solved))
        both = jnp.concatenate(halves, axis=0).T.astype(BF16)
        load_ref[:, pair] = both.reshape(levels, span, both.shape[1])


def operator_kernel(slot_ref, rows_ref, gain_ref, op_ref):
    senders, rows, lanes = op_ref.shape
    nodes, _, block = gain_ref.shape
    low = low_lanes((rows, lanes), rows)
    for s in range(senders):
        hot = (
            lax.broadcasted_iota(jnp.int32, (block, lanes), 0) == rows_ref[s : s + 1, :]
        ).astype(BF16)
        first = dot(gain_ref[jnp.minimum(slot_ref[2 * s], nodes - 1)], hot)
        second = dot(gain_ref[jnp.minimum(slot_ref[2 * s + 1], nodes - 1)], hot)
        op_ref[s] = jnp.where(low, first, second).astype(BF16)


def pack(values, take_ref, level, send_ref):
    senders, span, lanes = send_ref.shape
    low = low_lanes((span, lanes), lanes // 2)
    for d in range(senders):
        first = values[take_ref[level, 2 * d]]
        second = values[take_ref[level, 2 * d + 1]]
        send_ref[d] = jnp.where(low, first, second)


def both_halves(pair_value, odd, low, half):
    turned = pltpu.roll(pair_value, half, 1)
    return jnp.where(low, turned, pair_value) if odd else jnp.where(low, pair_value, turned)


def first_kernel(take_ref, load_ref, send_ref, values):
    pairs, span, lanes = load_ref.shape
    low = low_lanes((span, lanes), lanes // 2)
    for pair in range(pairs):
        value = load_ref[pair].astype(F32)
        for odd in (0, 1):
            values[2 * pair + odd] = both_halves(value, odd, low, lanes // 2).astype(BF16)
    values[2 * pairs] = jnp.zeros((span, lanes), BF16)
    pack(values, take_ref, 0, send_ref)


def hop_kernel(
    level, take_ref, slot_ref, got_ref, op_ref, load_ref, send_ref, ops, total, values, ready
):
    senders, span, lanes = got_ref.shape
    pairs = load_ref.shape[0]
    half = lanes // 2
    share = senders // ready.shape[0]
    copies = []
    for i in range(ready.shape[0]):
        where = pl.ds(i * share, share)
        copies.append(
            pltpu.make_async_copy(op_ref.at[level, where], ops.at[where], ready.at[i])
        )
        copies[-1].start()
    low = low_lanes((span, lanes), half)
    low_op = low_lanes((half, lanes), half)
    total[...] = jnp.zeros_like(total)
    for s in range(senders):
        if s % share == 0:
            copies[s // share].wait()
        op = ops[s]
        zero = jnp.zeros_like(op)
        split = jnp.concatenate(
            [jnp.where(low_op, op, zero), jnp.where(low_op, zero, op)], axis=0
        )
        part = dot_nt(got_ref[s], split)
        one = slot_ref[level - 1, 2 * s]
        two = slot_ref[level - 1, 2 * s + 1]
        total[one] += jnp.where(low, part, 0.0)
        total[two] += jnp.where(low, 0.0, part)
    for pair in range(pairs):
        value = load_ref[pair].astype(F32)
        for odd in (0, 1):
            node = 2 * pair + odd
            come = total[node]
            come = come + pltpu.roll(come, half, 1)
            values[node] = (both_halves(value, odd, low, half) - come).astype(BF16)
    values[2 * pairs] = jnp.zeros((span, lanes), BF16)
    pack(values, take_ref, level, send_ref)


def finish_kernel(
    early_counts,
    level_ref,
    slot_ref,
    rows_ref,
    rhs_ref,
    inv_ref,
    below_ref,
    *rest,
):
    chunks, parts = rest[-1].shape
    groups = len(early_counts)
    early = rest[:groups]
    sol_ref, out_ref, got, rhs, inv, below, inflow, base_ready, ready = rest[-9:]
    late = rest[groups:-9]
    late = [late[i : i + chunks] for i in range(0, len(late), chunks)]
    level = level_ref[0]
    step = pl.program_id(0)
    _, senders, span, lanes = got.shape
    _, nodes, block, _ = sol_ref.shape
    half = lanes // 2
    share = senders // parts
    spots = [pl.ds(p * share, share) for p in range(parts)]
    base = [
        pltpu.make_async_copy(source, target, base_ready.at[i])
        for i, (source, target) in enumerate(((rhs_ref, rhs), (inv_ref, inv), (below_ref, below)))
    ]

    @pl.when(step == 0)
    def _():
        def fetch(source):
            for p, spot in enumerate(spots):
                for c in range(chunks):
                    pltpu.make_async_copy(
                        source(c).at[spot], got.at[c, spot], ready.at[c, p]
                    ).start()

        reach = 1
        for index, (array, count) in enumerate(zip(early, early_counts)):
            inside = level < reach + count
            if index > 0:
                inside = jnp.logical_and(inside, level >= reach)

            @pl.when(inside)
            def _(array=array, reach=reach):
                fetch(lambda c: array.at[c, jnp.maximum(level - reach, 0)])

            reach += count
        for arrays in late:

            @pl.when(level == reach)
            def _(arrays=arrays):
                fetch(lambda c: arrays[c])

            reach += 1
        for copy in base:
            copy.start()

        inflow[...] = jnp.zeros_like(inflow)
        low = low_lanes((block, lanes), half)
        for s in range(senders):
            if s % share == 0:
                p = s // share
                for c in range(chunks):
                    pltpu.make_async_copy(
                        got.at[c, spots[p]], got.at[c, spots[p]], ready.at[c, p]
                    ).wait()
            hot = lax.broadcasted_iota(jnp.int32, (block, lanes), 0) == rows_ref[s : s + 1, :]
            hot = jnp.concatenate(
                [jnp.logical_and(hot, low), jnp.logical_and(hot, jnp.logical_not(low))], axis=0
            )
            part = dot(hot.astype(BF16), got[:, s].reshape(chunks * span, lanes).T)
            inflow[slot_ref[2 * s]] += part[:block]
            inflow[slot_ref[2 * s + 1]] += part[block:]
        for copy in base:
            copy.wait()

    @pl.when(step > 0)
    def _():
        at = (step - 1) * nodes
        reduced = [
            (rhs[at + n].astype(F32) - inflow[at + n]).astype(BF16) for n in range(nodes)
        ]
        solved = [dot(inv[at + n], reduced[n]).astype(BF16) for n in range(nodes)]
        for n in range(nodes):
            sol_ref[0, n] = solved[n]
        for n in range(nodes):
            out_ref[0, n] = dot(below[at + n], solved[n]).astype(BF16)


def params(limit, *semantics):
    return pltpu.CompilerParams(
        vmem_limit_bytes=limit * 1024 * 1024, dimension_semantics=semantics or None
    )


SMEM_SPEC = pl.BlockSpec(memory_space=pltpu.SMEM)
VMEM_SPEC = pl.BlockSpec(memory_space=pltpu.VMEM)
HBM_SPEC = pl.BlockSpec(memory_space=pltpu.HBM)


def shards(right_side, diag_inverse, below_block, parent_device, parent_slot, row_index):
    levels = lax.axis_size("level")
    group = lax.axis_size("grp")
    level_id = lax.axis_index("level")
    member = lax.axis_index("grp")
    _, nodes, block, columns = right_side.shape
    rows = below_block.shape[2]
    span = columns // levels
    lanes = 2 * rows
    pairs = nodes // 2
    hops = levels - 1

    step = 4
    gain, load = pl.pallas_call(
        prepare_kernel,
        grid=(nodes // step,),
        in_specs=[
            pl.BlockSpec((step, block, columns), lambda i: (i, 0, 0)),
            pl.BlockSpec((step, block, block), lambda i: (i, 0, 0)),
            pl.BlockSpec((step, rows, block), lambda i: (i, 0, 0)),
        ],
        out_specs=[
            pl.BlockSpec((step, rows, block), lambda i: (i, 0, 0)),
            pl.BlockSpec((levels, step // 2, span, lanes), lambda i: (0, i, 0, 0)),
        ],
        out_shape=[
            jax.ShapeDtypeStruct((nodes, rows, block), BF16),
            jax.ShapeDtypeStruct((levels, pairs, span, lanes), BF16),
        ],
        compiler_params=params(60, "arbitrary"),
        name="prepare",
    )(right_side[0], diag_inverse[0], below_block[0])

    devices = parent_device[:hops, :, 0].reshape(hops, group, nodes)
    slots = parent_slot[:hops].reshape(hops, group, nodes)
    place = lax.broadcasted_iota(jnp.int32, (hops, group, nodes), 2)

    def ends(named):
        first = jnp.min(jnp.where(named, place, nodes), axis=-1)
        last = jnp.max(jnp.where(named, place, -1), axis=-1)
        return first, jnp.where(last > first, last, nodes)

    first, last = ends(devices == member)
    own = lax.dynamic_index_in_dim(devices, member, 1, keepdims=True)
    take = jnp.stack(ends(own == lax.broadcasted_iota(jnp.int32, (hops, group, nodes), 1)), -1)
    take = take.reshape(hops, 2 * group)

    def slot_of(which):
        hit = place == which[..., None]
        found = jnp.sum(jnp.where(hit, slots, 0), axis=-1)
        return jnp.where(which < nodes, found, nodes)

    slot = jnp.stack([slot_of(first), slot_of(last)], -1).reshape(hops, 2 * group)

    before = jnp.maximum(level_id - 1, 0)
    home_slot = lax.dynamic_index_in_dim(slot, before, 0, keepdims=False)
    home_slot = jnp.where(level_id > 0, home_slot, nodes)
    landing = lax.dynamic_index_in_dim(row_index, before, 0, keepdims=False)
    landing = landing.reshape(rows, group, nodes)

    def rows_of(which):
        which = lax.dynamic_index_in_dim(which, before, 0, keepdims=False)[None, :, None]
        hit = lax.broadcasted_iota(jnp.int32, (rows, group, nodes), 2) == which
        found = jnp.sum(jnp.where(hit, landing, 0), axis=-1)
        return jnp.where(which[..., 0] < nodes, found, -1)

    home_rows = jnp.concatenate([rows_of(first), rows_of(last)], axis=0).T

    operators = pl.pallas_call(
        operator_kernel,
        in_specs=[SMEM_SPEC, VMEM_SPEC, VMEM_SPEC],
        out_specs=VMEM_SPEC,
        out_shape=jax.ShapeDtypeStruct((group, rows, lanes), BF16),
        compiler_params=params(16),
        name="operators",
    )(home_slot, home_rows, gain)
    operators = lax.all_gather(operators, "level", axis=0)
    loads = lax.all_to_all(load, "level", split_axis=0, concat_axis=0, tiled=True)

    message = jax.ShapeDtypeStruct((group, span, lanes), BF16)
    values_shape = pltpu.VMEM((nodes + 1, span, lanes), BF16)
    arrived = [None]
    early_counts = (hops // 2, hops - 1 - hops // 2)
    early = []
    for level in range(hops):
        if level == 0:
            send = pl.pallas_call(
                first_kernel,
                in_specs=[SMEM_SPEC, VMEM_SPEC],
                out_specs=VMEM_SPEC,
                out_shape=message,
                scratch_shapes=[values_shape],
                compiler_params=params(16),
                name="first",
            )(take, loads[0])
        else:
            send = pl.pallas_call(
                functools.partial(hop_kernel, level),
                in_specs=[SMEM_SPEC, SMEM_SPEC, VMEM_SPEC, HBM_SPEC, VMEM_SPEC],
                out_specs=VMEM_SPEC,
                out_shape=message,
                scratch_shapes=[
                    pltpu.VMEM((group, rows, lanes), BF16),
                    pltpu.VMEM((nodes + 1, span, lanes), F32),
                    values_shape,
                    pltpu.SemaphoreType.DMA((8,)),
                ],
                compiler_params=params(53),
                name="hop",
            )(take, slot, arrived[-1], operators, loads[level])
        arrived.append(lax.all_to_all(send, "grp", split_axis=0, concat_axis=0, tiled=True))
        if len(arrived) == 1 + sum(early_counts[: len(early) + 1]) and len(early) < 2:
            ready = jnp.stack(arrived[1 + sum(early_counts[: len(early)]) :])
            early.append(lax.all_gather(ready, "level", axis=0))
        elif len(arrived) == hops:
            arrived[-1], early[0] = lax.optimization_barrier((arrived[-1], early[0]))

    late = []
    for level in range(1 + sum(early_counts), levels):
        late += [
            arrived[level]
            if c == level
            else lax.ppermute(arrived[level], "level", [(c, level)])
            for c in range(levels)
        ]

    step = 8
    parts = 4
    tail = lambda i: jnp.maximum(i - 1, 0)
    return pl.pallas_call(
        functools.partial(finish_kernel, early_counts),
        grid=(1 + nodes // step,),
        in_specs=[SMEM_SPEC, SMEM_SPEC, VMEM_SPEC]
        + [HBM_SPEC] * (3 + len(early) + len(late)),
        out_specs=[
            pl.BlockSpec((1, step, block, columns), lambda i: (0, tail(i), 0, 0)),
            pl.BlockSpec((1, step, rows, columns), lambda i: (0, tail(i), 0, 0)),
        ],
        out_shape=[
            jax.ShapeDtypeStruct((1, nodes, block, columns), BF16),
            jax.ShapeDtypeStruct((1, nodes, rows, columns), BF16),
        ],
        scratch_shapes=[
            pltpu.VMEM((levels, group, span, lanes), BF16),
            pltpu.VMEM((nodes, block, columns), BF16),
            pltpu.VMEM((nodes, block, block), BF16),
            pltpu.VMEM((nodes, rows, block), BF16),
            pltpu.VMEM((nodes + 1, block, columns), F32),
            pltpu.SemaphoreType.DMA((3,)),
            pltpu.SemaphoreType.DMA((levels, parts)),
        ],
        compiler_params=params(58, "arbitrary"),
        name="finish",
    )(
        level_id.reshape(1),
        home_slot,
        home_rows,
        right_side[0],
        diag_inverse[0],
        below_block[0],
        *early,
        *late,
    )


def solution(mesh):
    return jax.shard_map(
        shards,
        mesh=mesh,
        in_specs=(
            P("level", "grp", None, None),
            P("level", "grp", None, None),
            P("level", "grp", None, None),
            P(),
            P(),
            P(),
        ),
        out_specs=(P("level", "grp", None, None), P("level", "grp", None, None)),
        check_vma=False,
    )
```

```python
import functools

import jax
import jax.numpy as jnp
from jax import lax
from jax.experimental import pallas as pl
from jax.experimental.pallas import tpu as pltpu
from jax.sharding import PartitionSpec as P

F32 = jnp.float32
BF16 = jnp.bfloat16


def dot(a, b):
    return jnp.dot(a, b, preferred_element_type=F32)


def dot_nt(a, b):
    return lax.dot_general(a, b, (((1,), (1,)), ((), ())), preferred_element_type=F32)


def low_lanes(shape, half):
    return lax.broadcasted_iota(jnp.int32, shape, len(shape) - 1) < half


def prepare_kernel(
    slot_ref,
    rows_ref,
    rhs_ref,
    inv_ref,
    below_ref,
    op_ref,
    load_ref,
    rhs,
    inv,
    below,
    gain,
    op,
    load,
    ready,
    done,
):
    nodes, rows, block = below.shape
    levels, pairs, span, lanes = load.shape
    senders = op.shape[0]
    parts = ready.shape[1]
    share = nodes // parts
    spots = [pl.ds(p * share, share) for p in range(parts)]
    coming = [
        [
            pltpu.make_async_copy(source.at[spot], target.at[spot], ready.at[i, p])
            for p, spot in enumerate(spots)
        ]
        for i, (source, target) in enumerate(((inv_ref, inv), (below_ref, below), (rhs_ref, rhs)))
    ]
    for first, second in zip(coming[0], coming[1]):
        first.start()
        second.start()
    for copy in coming[2]:
        copy.start()
    going = [pltpu.make_async_copy(op, op_ref, done.at[0])]
    for p in range(parts):
        spot = pl.ds(p * share // 2, share // 2)
        going.append(
            pltpu.make_async_copy(load.at[:, spot], load_ref.at[:, spot], done.at[1 + p])
        )

    for p in range(parts):
        coming[0][p].wait()
        coming[1][p].wait()
        for node in range(p * share, (p + 1) * share):
            gain[node] = dot(below[node], inv[node]).astype(BF16)
    low = low_lanes((rows, lanes), rows)
    for s in range(senders):
        hot = (
            lax.broadcasted_iota(jnp.int32, (block, lanes), 0) == rows_ref[s : s + 1, :]
        ).astype(BF16)
        one = dot(gain[jnp.minimum(slot_ref[2 * s], nodes - 1)], hot)
        two = dot(gain[jnp.minimum(slot_ref[2 * s + 1], nodes - 1)], hot)
        op[s] = jnp.where(low, one, two).astype(BF16)
    going[0].start()
    for p in range(parts):
        coming[2][p].wait()
        mine = range(p * share, (p + 1) * share)
        solved = [dot(inv[node], rhs[node]).astype(BF16) for node in mine]
        updates = [dot(below[node], value) for node, value in zip(mine, solved)]
        for i in range(0, share, 2):
            both = jnp.concatenate(updates[i : i + 2], axis=0).T.astype(BF16)
            load[:, (p * share + i) // 2] = both.reshape(levels, span, lanes)
        going[1 + p].start()
    for copy in going:
        copy.wait()


def pack(values, take_ref, level, send_ref):
    senders, span, lanes = send_ref.shape
    low = low_lanes((span, lanes), lanes // 2)
    for d in range(senders):
        first = values[take_ref[level, 2 * d]]
        second = values[take_ref[level, 2 * d + 1]]
        send_ref[d] = jnp.where(low, first, second)


def both_halves(pair_value, odd, low, half):
    turned = pltpu.roll(pair_value, half, 1)
    return jnp.where(low, turned, pair_value) if odd else jnp.where(low, pair_value, turned)


def first_kernel(take_ref, load_ref, send_ref, values):
    _, pairs, span, lanes = load_ref.shape
    low = low_lanes((span, lanes), lanes // 2)
    for pair in range(pairs):
        value = load_ref[0, pair].astype(F32)
        for odd in (0, 1):
            values[2 * pair + odd] = both_halves(value, odd, low, lanes // 2).astype(BF16)
    values[2 * pairs] = jnp.zeros((span, lanes), BF16)
    pack(values, take_ref, 0, send_ref)


def hop_kernel(
    level,
    take_ref,
    slot_ref,
    got_ref,
    all_op_ref,
    all_load_ref,
    send_ref,
    ops,
    load,
    total,
    values,
    ready,
    loaded,
):
    senders, span, lanes = got_ref.shape
    pairs = load.shape[0]
    half = lanes // 2
    parts = ready.shape[0]
    share = senders // parts
    copies = [
        pltpu.make_async_copy(
            all_op_ref.at[level, pl.ds(i * share, share)],
            ops.at[pl.ds(i * share, share)],
            ready.at[i],
        )
        for i in range(parts)
    ]
    for copy in copies:
        copy.start()
    loading = pltpu.make_async_copy(all_load_ref.at[level], load, loaded.at[0])
    loading.start()
    low = low_lanes((span, lanes), half)
    low_op = low_lanes((half, lanes), half)
    total[...] = jnp.zeros_like(total)
    for s in range(senders):
        if s == 0:
            for copy in copies[: parts // 2]:
                copy.wait()
        elif s == senders // 2:
            for copy in copies[parts // 2 :]:
                copy.wait()
        op = ops[s]
        zero = jnp.zeros_like(op)
        split = jnp.concatenate(
            [jnp.where(low_op, op, zero), jnp.where(low_op, zero, op)], axis=0
        )
        part = dot_nt(got_ref[s], split)
        one = slot_ref[level - 1, 2 * s]
        two = slot_ref[level - 1, 2 * s + 1]
        total[one] += jnp.where(low, part, 0.0)
        total[two] += jnp.where(low, 0.0, part)
    loading.wait()
    for pair in range(pairs):
        value = load[pair].astype(F32)
        for odd in (0, 1):
            node = 2 * pair + odd
            come = total[node]
            come = come + pltpu.roll(come, half, 1)
            values[node] = (both_halves(value, odd, low, half) - come).astype(BF16)
    values[2 * pairs] = jnp.zeros((span, lanes), BF16)
    pack(values, take_ref, level, send_ref)


def finish_kernel(
    early_counts,
    level_ref,
    slot_ref,
    rows_ref,
    rhs_ref,
    inv_ref,
    below_ref,
    *rest,
):
    chunks, parts = rest[-1].shape
    groups = len(early_counts)
    early = rest[:groups]
    sol_ref, out_ref, got, rhs, inv, below, inflow, base_ready, ready = rest[-9:]
    late = rest[groups:-9]
    late = [late[i : i + chunks] for i in range(0, len(late), chunks)]
    level = level_ref[0]
    step = pl.program_id(0)
    _, senders, span, lanes = got.shape
    _, nodes, block, _ = sol_ref.shape
    half = lanes // 2
    share = senders // parts
    spots = [pl.ds(p * share, share) for p in range(parts)]
    base = [
        pltpu.make_async_copy(source, target, base_ready.at[i])
        for i, (source, target) in enumerate(((rhs_ref, rhs), (inv_ref, inv), (below_ref, below)))
    ]

    @pl.when(step == 0)
    def _():
        def fetch(source):
            for p, spot in enumerate(spots):
                for c in range(chunks):
                    pltpu.make_async_copy(
                        source(c).at[spot], got.at[c, spot], ready.at[c, p]
                    ).start()

        reach = 1
        for index, (array, count) in enumerate(zip(early, early_counts)):
            inside = level < reach + count
            if index > 0:
                inside = jnp.logical_and(inside, level >= reach)

            @pl.when(inside)
            def _(array=array, reach=reach):
                fetch(lambda c: array.at[c, jnp.maximum(level - reach, 0)])

            reach += count
        for arrays in late:

            @pl.when(level == reach)
            def _(arrays=arrays):
                fetch(lambda c: arrays[c])

            reach += 1
        for copy in base:
            copy.start()

        inflow[...] = jnp.zeros_like(inflow)
        low = low_lanes((block, lanes), half)
        for s in range(senders):
            if s % share == 0:
                p = s // share
                for c in range(chunks):
                    pltpu.make_async_copy(
                        got.at[c, spots[p]], got.at[c, spots[p]], ready.at[c, p]
                    ).wait()
            hot = lax.broadcasted_iota(jnp.int32, (block, lanes), 0) == rows_ref[s : s + 1, :]
            hot = jnp.concatenate(
                [jnp.logical_and(hot, low), jnp.logical_and(hot, jnp.logical_not(low))], axis=0
            )
            part = dot(hot.astype(BF16), got[:, s].reshape(chunks * span, lanes).T)
            inflow[slot_ref[2 * s]] += part[:block]
            inflow[slot_ref[2 * s + 1]] += part[block:]
        for copy in base:
            copy.wait()

    @pl.when(step > 0)
    def _():
        at = (step - 1) * nodes
        reduced = [
            (rhs[at + n].astype(F32) - inflow[at + n]).astype(BF16) for n in range(nodes)
        ]
        solved = [dot(inv[at + n], reduced[n]).astype(BF16) for n in range(nodes)]
        for n in range(nodes):
            sol_ref[0, n] = solved[n]
        for n in range(nodes):
            out_ref[0, n] = dot(below[at + n], solved[n]).astype(BF16)


def params(limit, *semantics):
    return pltpu.CompilerParams(
        vmem_limit_bytes=limit * 1024 * 1024, dimension_semantics=semantics or None
    )


SMEM_SPEC = pl.BlockSpec(memory_space=pltpu.SMEM)
VMEM_SPEC = pl.BlockSpec(memory_space=pltpu.VMEM)
HBM_SPEC = pl.BlockSpec(memory_space=pltpu.HBM)


def shards(right_side, diag_inverse, below_block, parent_device, parent_slot, row_index):
    levels = lax.axis_size("level")
    group = lax.axis_size("grp")
    level_id = lax.axis_index("level")
    member = lax.axis_index("grp")
    _, nodes, block, columns = right_side.shape
    rows = below_block.shape[2]
    span = columns // levels
    lanes = 2 * rows
    pairs = nodes // 2
    hops = levels - 1

    devices = parent_device[:hops, :, 0].reshape(hops, group, nodes)
    slots = parent_slot[:hops].reshape(hops, group, nodes)
    place = lax.broadcasted_iota(jnp.int32, (hops, group, nodes), 2)

    def ends(named):
        first = jnp.min(jnp.where(named, place, nodes), axis=-1)
        last = jnp.max(jnp.where(named, place, -1), axis=-1)
        return first, jnp.where(last > first, last, nodes)

    first, last = ends(devices == member)
    own = lax.dynamic_index_in_dim(devices, member, 1, keepdims=True)
    take = jnp.stack(ends(own == lax.broadcasted_iota(jnp.int32, (hops, group, nodes), 1)), -1)
    take = take.reshape(hops, 2 * group)

    def slot_of(which):
        hit = place == which[..., None]
        found = jnp.sum(jnp.where(hit, slots, 0), axis=-1)
        return jnp.where(which < nodes, found, nodes)

    slot = jnp.stack([slot_of(first), slot_of(last)], -1).reshape(hops, 2 * group)

    before = jnp.maximum(level_id - 1, 0)
    home_slot = lax.dynamic_index_in_dim(slot, before, 0, keepdims=False)
    home_slot = jnp.where(level_id > 0, home_slot, nodes)
    landing = lax.dynamic_index_in_dim(row_index, before, 0, keepdims=False)
    landing = landing.reshape(rows, group, nodes)

    def rows_of(which):
        which = lax.dynamic_index_in_dim(which, before, 0, keepdims=False)[None, :, None]
        hit = lax.broadcasted_iota(jnp.int32, (rows, group, nodes), 2) == which
        found = jnp.sum(jnp.where(hit, landing, 0), axis=-1)
        return jnp.where(which[..., 0] < nodes, found, -1)

    home_rows = jnp.concatenate([rows_of(first), rows_of(last)], axis=0).T

    parts = 4
    operators, load = pl.pallas_call(
        prepare_kernel,
        in_specs=[SMEM_SPEC, VMEM_SPEC, HBM_SPEC, HBM_SPEC, HBM_SPEC],
        out_specs=[HBM_SPEC, HBM_SPEC],
        out_shape=[
            jax.ShapeDtypeStruct((group, rows, lanes), BF16),
            jax.ShapeDtypeStruct((levels, pairs, span, lanes), BF16),
        ],
        scratch_shapes=[
            pltpu.VMEM((nodes, block, columns), BF16),
            pltpu.VMEM((nodes, block, block), BF16),
            pltpu.VMEM((nodes, rows, block), BF16),
            pltpu.VMEM((nodes, rows, block), BF16),
            pltpu.VMEM((group, rows, lanes), BF16),
            pltpu.VMEM((levels, pairs, span, lanes), BF16),
            pltpu.SemaphoreType.DMA((3, parts)),
            pltpu.SemaphoreType.DMA((1 + parts,)),
        ],
        compiler_params=params(58),
        name="prepare",
    )(home_slot, home_rows, right_side[0], diag_inverse[0], below_block[0])
    operators = lax.all_gather(operators, "level", axis=0)
    loads = lax.all_to_all(load, "level", split_axis=0, concat_axis=0, tiled=True)

    message = jax.ShapeDtypeStruct((group, span, lanes), BF16)
    values_shape = pltpu.VMEM((nodes + 1, span, lanes), BF16)
    arrived = [None]
    early_counts = (hops // 2, hops - 1 - hops // 2)
    early = []
    for level in range(hops):
        if level == 0:
            send = pl.pallas_call(
                first_kernel,
                in_specs=[SMEM_SPEC, VMEM_SPEC],
                out_specs=VMEM_SPEC,
                out_shape=message,
                scratch_shapes=[values_shape],
                compiler_params=params(16),
                name="first",
            )(take, loads)
        else:
            send = pl.pallas_call(
                functools.partial(hop_kernel, level),
                in_specs=[SMEM_SPEC, SMEM_SPEC, VMEM_SPEC, HBM_SPEC, HBM_SPEC],
                out_specs=VMEM_SPEC,
                out_shape=message,
                scratch_shapes=[
                    pltpu.VMEM((group, rows, lanes), BF16),
                    pltpu.VMEM((pairs, span, lanes), BF16),
                    pltpu.VMEM((nodes + 1, span, lanes), F32),
                    values_shape,
                    pltpu.SemaphoreType.DMA((8,)),
                    pltpu.SemaphoreType.DMA((1,)),
                ],
                compiler_params=params(53),
                name="hop",
            )(take, slot, arrived[-1], operators, loads)
        arrived.append(lax.all_to_all(send, "grp", split_axis=0, concat_axis=0, tiled=True))
        if len(arrived) == 1 + sum(early_counts[: len(early) + 1]) and len(early) < 2:
            ready = jnp.stack(arrived[1 + sum(early_counts[: len(early)]) :])
            early.append(lax.all_gather(ready, "level", axis=0))
        elif len(arrived) == hops:
            arrived[-1], early[0] = lax.optimization_barrier((arrived[-1], early[0]))

    late = []
    for level in range(1 + sum(early_counts), levels):
        late += [
            arrived[level]
            if c == level
            else lax.ppermute(arrived[level], "level", [(c, level)])
            for c in range(levels)
        ]

    step = 8
    tail = lambda i: jnp.maximum(i - 1, 0)
    return pl.pallas_call(
        functools.partial(finish_kernel, early_counts),
        grid=(1 + nodes // step,),
        in_specs=[SMEM_SPEC, SMEM_SPEC, VMEM_SPEC]
        + [HBM_SPEC] * (3 + len(early) + len(late)),
        out_specs=[
            pl.BlockSpec((1, step, block, columns), lambda i: (0, tail(i), 0, 0)),
            pl.BlockSpec((1, step, rows, columns), lambda i: (0, tail(i), 0, 0)),
        ],
        out_shape=[
            jax.ShapeDtypeStruct((1, nodes, block, columns), BF16),
            jax.ShapeDtypeStruct((1, nodes, rows, columns), BF16),
        ],
        scratch_shapes=[
            pltpu.VMEM((levels, group, span, lanes), BF16),
            pltpu.VMEM((nodes, block, columns), BF16),
            pltpu.VMEM((nodes, block, block), BF16),
            pltpu.VMEM((nodes, rows, block), BF16),
            pltpu.VMEM((nodes + 1, block, columns), F32),
            pltpu.SemaphoreType.DMA((3,)),
            pltpu.SemaphoreType.DMA((levels, parts)),
        ],
        compiler_params=params(58, "arbitrary"),
        name="finish",
    )(
        level_id.reshape(1),
        home_slot,
        home_rows,
        right_side[0],
        diag_inverse[0],
        below_block[0],
        *early,
        *late,
    )


def solution(mesh):
    return jax.shard_map(
        shards,
        mesh=mesh,
        in_specs=(
            P("level", "grp", None, None),
            P("level", "grp", None, None),
            P("level", "grp", None, None),
            P(),
            P(),
            P(),
        ),
        out_specs=(P("level", "grp", None, None), P("level", "grp", None, None)),
        check_vma=False,
    )
```

```python
import functools

import jax
import jax.numpy as jnp
from jax import lax
from jax.experimental import pallas as pl
from jax.experimental.pallas import tpu as pltpu
from jax.sharding import PartitionSpec as P

F32 = jnp.float32
BF16 = jnp.bfloat16


def dot(a, b):
    return jnp.dot(a, b, preferred_element_type=F32)


def dot_nt(a, b):
    return lax.dot_general(a, b, (((1,), (1,)), ((), ())), preferred_element_type=F32)


def low_lanes(shape, half):
    return lax.broadcasted_iota(jnp.int32, shape, len(shape) - 1) < half


def prepare_kernel(
    slot_ref,
    rows_ref,
    rhs_ref,
    inv_ref,
    below_ref,
    op_ref,
    load_ref,
    rhs,
    inv,
    below,
    gain,
    op,
    load,
    ready,
    done,
):
    nodes, rows, block = below.shape
    levels, pairs, span, lanes = load.shape
    senders = op.shape[0]
    parts = ready.shape[1]
    share = nodes // parts
    spots = [pl.ds(p * share, share) for p in range(parts)]
    coming = [
        [
            pltpu.make_async_copy(source.at[spot], target.at[spot], ready.at[i, p])
            for p, spot in enumerate(spots)
        ]
        for i, (source, target) in enumerate(((inv_ref, inv), (below_ref, below), (rhs_ref, rhs)))
    ]
    for first, second in zip(coming[0], coming[1]):
        first.start()
        second.start()
    for copy in coming[2]:
        copy.start()
    going = [pltpu.make_async_copy(op, op_ref, done.at[0])]
    for p in range(parts):
        spot = pl.ds(p * share // 2, share // 2)
        going.append(
            pltpu.make_async_copy(load.at[:, spot], load_ref.at[:, spot], done.at[1 + p])
        )

    for p in range(parts):
        coming[0][p].wait()
        coming[1][p].wait()
        for node in range(p * share, (p + 1) * share):
            gain[node] = dot(below[node], inv[node]).astype(BF16)
    low = low_lanes((rows, lanes), rows)
    for s in range(senders):
        hot = (
            lax.broadcasted_iota(jnp.int32, (block, lanes), 0) == rows_ref[s : s + 1, :]
        ).astype(BF16)
        one = dot(gain[jnp.minimum(slot_ref[2 * s], nodes - 1)], hot)
        two = dot(gain[jnp.minimum(slot_ref[2 * s + 1], nodes - 1)], hot)
        op[s] = jnp.where(low, one, two).astype(BF16)
    going[0].start()
    for p in range(parts):
        coming[2][p].wait()
        mine = range(p * share, (p + 1) * share)
        solved = [dot(inv[node], rhs[node]).astype(BF16) for node in mine]
        updates = [dot(below[node], value) for node, value in zip(mine, solved)]
        for i in range(0, share, 2):
            both = jnp.concatenate(updates[i : i + 2], axis=0).T.astype(BF16)
            load[:, (p * share + i) // 2] = both.reshape(levels, span, lanes)
        going[1 + p].start()
    for copy in going:
        copy.wait()


def pack(values, take_ref, level, send_ref):
    senders, span, lanes = send_ref.shape
    low = low_lanes((span, lanes), lanes // 2)
    for d in range(senders):
        first = values[take_ref[level, 2 * d]]
        second = values[take_ref[level, 2 * d + 1]]
        send_ref[d] = jnp.where(low, first, second)


def both_halves(pair_value, odd, low, half):
    turned = pltpu.roll(pair_value, half, 1)
    return jnp.where(low, turned, pair_value) if odd else jnp.where(low, pair_value, turned)


def first_kernel(take_ref, load_ref, send_ref, values):
    _, pairs, span, lanes = load_ref.shape
    low = low_lanes((span, lanes), lanes // 2)
    for pair in range(pairs):
        value = load_ref[0, pair].astype(F32)
        for odd in (0, 1):
            values[2 * pair + odd] = both_halves(value, odd, low, lanes // 2).astype(BF16)
    values[2 * pairs] = jnp.zeros((span, lanes), BF16)
    pack(values, take_ref, 0, send_ref)


def hop_kernel(
    level,
    have,
    ahead,
    take_ref,
    slot_ref,
    got_ref,
    all_op_ref,
    all_load_ref,
    *rest,
):
    ops, load, total, values, ready, loaded = rest[-6:]
    send_ref = rest[1] if have else rest[0]
    senders, span, lanes = got_ref.shape
    pairs = load.shape[0]
    half = lanes // 2
    parts = ready.shape[0]
    share = senders // parts

    def bring(source, target):
        return [
            pltpu.make_async_copy(
                source.at[pl.ds(i * share, share)],
                target.at[pl.ds(i * share, share)],
                ready.at[i],
            )
            for i in range(parts)
        ]

    copies, following = [], []
    if have:
        ops = rest[0]
    else:
        copies = bring(all_op_ref.at[level], ops)
    if ahead:
        following = bring(all_op_ref.at[level + 1], rest[-7])
    for copy in copies if copies else following:
        copy.start()
    loading = pltpu.make_async_copy(all_load_ref.at[level], load, loaded.at[0])
    loading.start()
    low = low_lanes((span, lanes), half)
    low_op = low_lanes((half, lanes), half)
    total[...] = jnp.zeros_like(total)
    for s in range(senders):
        if s == 0:
            for copy in copies[: parts // 2]:
                copy.wait()
        elif s == senders // 2:
            for copy in copies[parts // 2 :]:
                copy.wait()
            for copy in following if copies else []:
                copy.start()
        op = ops[s]
        zero = jnp.zeros_like(op)
        split = jnp.concatenate(
            [jnp.where(low_op, op, zero), jnp.where(low_op, zero, op)], axis=0
        )
        part = dot_nt(got_ref[s], split)
        one = slot_ref[level - 1, 2 * s]
        two = slot_ref[level - 1, 2 * s + 1]
        total[one] += jnp.where(low, part, 0.0)
        total[two] += jnp.where(low, 0.0, part)
    loading.wait()
    for pair in range(pairs):
        value = load[pair].astype(F32)
        for odd in (0, 1):
            node = 2 * pair + odd
            come = total[node]
            come = come + pltpu.roll(come, half, 1)
            values[node] = (both_halves(value, odd, low, half) - come).astype(BF16)
    values[2 * pairs] = jnp.zeros((span, lanes), BF16)
    pack(values, take_ref, level, send_ref)
    for copy in following:
        copy.wait()


def finish_kernel(
    early_counts,
    level_ref,
    slot_ref,
    rows_ref,
    rhs_ref,
    inv_ref,
    below_ref,
    *rest,
):
    chunks, parts = rest[-1].shape
    groups = len(early_counts)
    early = rest[:groups]
    sol_ref, out_ref, got, rhs, inv, below, inflow, base_ready, ready = rest[-9:]
    late = rest[groups:-9]
    late = [late[i : i + chunks] for i in range(0, len(late), chunks)]
    level = level_ref[0]
    step = pl.program_id(0)
    _, senders, span, lanes = got.shape
    _, nodes, block, _ = sol_ref.shape
    half = lanes // 2
    share = senders // parts
    spots = [pl.ds(p * share, share) for p in range(parts)]
    base = [
        pltpu.make_async_copy(source, target, base_ready.at[i])
        for i, (source, target) in enumerate(((rhs_ref, rhs), (inv_ref, inv), (below_ref, below)))
    ]

    @pl.when(step == 0)
    def _():
        def fetch(source):
            for p, spot in enumerate(spots):
                for c in range(chunks):
                    pltpu.make_async_copy(
                        source(c).at[spot], got.at[c, spot], ready.at[c, p]
                    ).start()

        reach = 1
        for index, (array, count) in enumerate(zip(early, early_counts)):
            inside = level < reach + count
            if index > 0:
                inside = jnp.logical_and(inside, level >= reach)

            @pl.when(inside)
            def _(array=array, reach=reach):
                fetch(lambda c: array.at[c, jnp.maximum(level - reach, 0)])

            reach += count
        for arrays in late:

            @pl.when(level == reach)
            def _(arrays=arrays):
                fetch(lambda c: arrays[c])

            reach += 1
        for copy in base:
            copy.start()

        inflow[...] = jnp.zeros_like(inflow)
        low = low_lanes((block, lanes), half)
        for s in range(senders):
            if s % share == 0:
                p = s // share
                for c in range(chunks):
                    pltpu.make_async_copy(
                        got.at[c, spots[p]], got.at[c, spots[p]], ready.at[c, p]
                    ).wait()
            hot = lax.broadcasted_iota(jnp.int32, (block, lanes), 0) == rows_ref[s : s + 1, :]
            hot = jnp.concatenate(
                [jnp.logical_and(hot, low), jnp.logical_and(hot, jnp.logical_not(low))], axis=0
            )
            part = dot(hot.astype(BF16), got[:, s].reshape(chunks * span, lanes).T)
            inflow[slot_ref[2 * s]] += part[:block]
            inflow[slot_ref[2 * s + 1]] += part[block:]
        for copy in base:
            copy.wait()

    @pl.when(step > 0)
    def _():
        at = (step - 1) * nodes
        reduced = [
            (rhs[at + n].astype(F32) - inflow[at + n]).astype(BF16) for n in range(nodes)
        ]
        solved = [dot(inv[at + n], reduced[n]).astype(BF16) for n in range(nodes)]
        for n in range(nodes):
            sol_ref[0, n] = solved[n]
        for n in range(nodes):
            out_ref[0, n] = dot(below[at + n], solved[n]).astype(BF16)


def params(limit, *semantics):
    return pltpu.CompilerParams(
        vmem_limit_bytes=limit * 1024 * 1024, dimension_semantics=semantics or None
    )


SMEM_SPEC = pl.BlockSpec(memory_space=pltpu.SMEM)
VMEM_SPEC = pl.BlockSpec(memory_space=pltpu.VMEM)
HBM_SPEC = pl.BlockSpec(memory_space=pltpu.HBM)


def shards(right_side, diag_inverse, below_block, parent_device, parent_slot, row_index):
    levels = lax.axis_size("level")
    group = lax.axis_size("grp")
    level_id = lax.axis_index("level")
    member = lax.axis_index("grp")
    _, nodes, block, columns = right_side.shape
    rows = below_block.shape[2]
    span = columns // levels
    lanes = 2 * rows
    pairs = nodes // 2
    hops = levels - 1

    devices = parent_device[:hops, :, 0].reshape(hops, group, nodes)
    slots = parent_slot[:hops].reshape(hops, group, nodes)
    place = lax.broadcasted_iota(jnp.int32, (hops, group, nodes), 2)

    def ends(named):
        first = jnp.min(jnp.where(named, place, nodes), axis=-1)
        last = jnp.max(jnp.where(named, place, -1), axis=-1)
        return first, jnp.where(last > first, last, nodes)

    first, last = ends(devices == member)
    own = lax.dynamic_index_in_dim(devices, member, 1, keepdims=True)
    take = jnp.stack(ends(own == lax.broadcasted_iota(jnp.int32, (hops, group, nodes), 1)), -1)
    take = take.reshape(hops, 2 * group)

    def slot_of(which):
        hit = place == which[..., None]
        found = jnp.sum(jnp.where(hit, slots, 0), axis=-1)
        return jnp.where(which < nodes, found, nodes)

    slot = jnp.stack([slot_of(first), slot_of(last)], -1).reshape(hops, 2 * group)

    before = jnp.maximum(level_id - 1, 0)
    home_slot = lax.dynamic_index_in_dim(slot, before, 0, keepdims=False)
    home_slot = jnp.where(level_id > 0, home_slot, nodes)
    landing = lax.dynamic_index_in_dim(row_index, before, 0, keepdims=False)
    landing = landing.reshape(rows, group, nodes)

    def rows_of(which):
        which = lax.dynamic_index_in_dim(which, before, 0, keepdims=False)[None, :, None]
        hit = lax.broadcasted_iota(jnp.int32, (rows, group, nodes), 2) == which
        found = jnp.sum(jnp.where(hit, landing, 0), axis=-1)
        return jnp.where(which[..., 0] < nodes, found, -1)

    home_rows = jnp.concatenate([rows_of(first), rows_of(last)], axis=0).T

    parts = 4
    operators, load = pl.pallas_call(
        prepare_kernel,
        in_specs=[SMEM_SPEC, VMEM_SPEC, HBM_SPEC, HBM_SPEC, HBM_SPEC],
        out_specs=[HBM_SPEC, HBM_SPEC],
        out_shape=[
            jax.ShapeDtypeStruct((group, rows, lanes), BF16),
            jax.ShapeDtypeStruct((levels, pairs, span, lanes), BF16),
        ],
        scratch_shapes=[
            pltpu.VMEM((nodes, block, columns), BF16),
            pltpu.VMEM((nodes, block, block), BF16),
            pltpu.VMEM((nodes, rows, block), BF16),
            pltpu.VMEM((nodes, rows, block), BF16),
            pltpu.VMEM((group, rows, lanes), BF16),
            pltpu.VMEM((levels, pairs, span, lanes), BF16),
            pltpu.SemaphoreType.DMA((3, parts)),
            pltpu.SemaphoreType.DMA((1 + parts,)),
        ],
        compiler_params=params(58),
        name="prepare",
    )(home_slot, home_rows, right_side[0], diag_inverse[0], below_block[0])
    operators = lax.all_gather(operators, "level", axis=0)
    loads = lax.all_to_all(load, "level", split_axis=0, concat_axis=0, tiled=True)

    message = jax.ShapeDtypeStruct((group, span, lanes), BF16)
    values_shape = pltpu.VMEM((nodes + 1, span, lanes), BF16)
    arrived = [None]
    brought = (2, 4, 5)
    following = []
    early_counts = (hops // 2, hops - 1 - hops // 2)
    early = []
    for level in range(hops):
        if level == 0:
            send = pl.pallas_call(
                first_kernel,
                in_specs=[SMEM_SPEC, VMEM_SPEC],
                out_specs=VMEM_SPEC,
                out_shape=message,
                scratch_shapes=[values_shape],
                compiler_params=params(16),
                name="first",
            )(take, loads)
        else:
            have, ahead = level in brought, level + 1 in brought
            operator = jax.ShapeDtypeStruct((group, rows, lanes), BF16)
            send, *following = pl.pallas_call(
                functools.partial(hop_kernel, level, have, ahead),
                in_specs=[SMEM_SPEC, SMEM_SPEC, VMEM_SPEC, HBM_SPEC, HBM_SPEC]
                + [VMEM_SPEC] * have,
                out_specs=[VMEM_SPEC] * (1 + ahead),
                out_shape=[message] + [operator] * ahead,
                scratch_shapes=[
                    pltpu.VMEM((group, rows, lanes), BF16),
                    pltpu.VMEM((pairs, span, lanes), BF16),
                    pltpu.VMEM((nodes + 1, span, lanes), F32),
                    values_shape,
                    pltpu.SemaphoreType.DMA((8,)),
                    pltpu.SemaphoreType.DMA((1,)),
                ],
                compiler_params=params(51),
                name="hop",
            )(take, slot, arrived[-1], operators, loads, *following)
        arrived.append(lax.all_to_all(send, "grp", split_axis=0, concat_axis=0, tiled=True))
        if len(arrived) == 1 + sum(early_counts[: len(early) + 1]) and len(early) < 2:
            ready = jnp.stack(arrived[1 + sum(early_counts[: len(early)]) :])
            early.append(lax.all_gather(ready, "level", axis=0))
        elif len(arrived) == hops:
            arrived[-1], early[0] = lax.optimization_barrier((arrived[-1], early[0]))

    late = []
    for level in range(1 + sum(early_counts), levels):
        late += [
            arrived[level]
            if c == level
            else lax.ppermute(arrived[level], "level", [(c, level)])
            for c in range(levels)
        ]

    step = 16
    tail = lambda i: jnp.maximum(i - 1, 0)
    return pl.pallas_call(
        functools.partial(finish_kernel, early_counts),
        grid=(1 + nodes // step,),
        in_specs=[SMEM_SPEC, SMEM_SPEC, VMEM_SPEC]
        + [HBM_SPEC] * (3 + len(early) + len(late)),
        out_specs=[
            pl.BlockSpec((1, step, block, columns), lambda i: (0, tail(i), 0, 0)),
            pl.BlockSpec((1, step, rows, columns), lambda i: (0, tail(i), 0, 0)),
        ],
        out_shape=[
            jax.ShapeDtypeStruct((1, nodes, block, columns), BF16),
            jax.ShapeDtypeStruct((1, nodes, rows, columns), BF16),
        ],
        scratch_shapes=[
            pltpu.VMEM((levels, group, span, lanes), BF16),
            pltpu.VMEM((nodes, block, columns), BF16),
            pltpu.VMEM((nodes, block, block), BF16),
            pltpu.VMEM((nodes, rows, block), BF16),
            pltpu.VMEM((nodes + 1, block, columns), F32),
            pltpu.SemaphoreType.DMA((3,)),
            pltpu.SemaphoreType.DMA((levels, 2)),
        ],
        compiler_params=params(58, "arbitrary"),
        name="finish",
    )(
        level_id.reshape(1),
        home_slot,
        home_rows,
        right_side[0],
        diag_inverse[0],
        below_block[0],
        *early,
        *late,
    )


def solution(mesh):
    return jax.shard_map(
        shards,
        mesh=mesh,
        in_specs=(
            P("level", "grp", None, None),
            P("level", "grp", None, None),
            P("level", "grp", None, None),
            P(),
            P(),
            P(),
        ),
        out_specs=(P("level", "grp", None, None), P("level", "grp", None, None)),
        check_vma=False,
    )
```

```python
import functools

import jax
import jax.numpy as jnp
from jax import lax
from jax.experimental import pallas as pl
from jax.experimental.pallas import tpu as pltpu
from jax.sharding import PartitionSpec as P

F32 = jnp.float32
BF16 = jnp.bfloat16


def dot(a, b):
    return jnp.dot(a, b, preferred_element_type=F32)


def dot_nt(a, b):
    return lax.dot_general(a, b, (((1,), (1,)), ((), ())), preferred_element_type=F32)


def low_lanes(shape, half):
    return lax.broadcasted_iota(jnp.int32, shape, len(shape) - 1) < half


def prepare_kernel(
    slot_ref,
    rows_ref,
    rhs_ref,
    inv_ref,
    below_ref,
    op_ref,
    load_ref,
    rhs,
    inv,
    below,
    gain,
    op,
    load,
    ready,
    done,
):
    nodes, rows, block = below.shape
    levels, pairs, span, lanes = load.shape
    senders = op.shape[0]
    parts = ready.shape[1]
    share = nodes // parts
    spots = [pl.ds(p * share, share) for p in range(parts)]
    coming = [
        [
            pltpu.make_async_copy(source.at[spot], target.at[spot], ready.at[i, p])
            for p, spot in enumerate(spots)
        ]
        for i, (source, target) in enumerate(((inv_ref, inv), (below_ref, below), (rhs_ref, rhs)))
    ]
    for first, second in zip(coming[0], coming[1]):
        first.start()
        second.start()
    for copy in coming[2]:
        copy.start()
    going = [pltpu.make_async_copy(op, op_ref, done.at[0])]
    for p in range(parts):
        spot = pl.ds(p * share // 2, share // 2)
        going.append(
            pltpu.make_async_copy(load.at[:, spot], load_ref.at[:, spot], done.at[1 + p])
        )

    for p in range(parts):
        coming[0][p].wait()
        coming[1][p].wait()
        for node in range(p * share, (p + 1) * share):
            gain[node] = dot(below[node], inv[node]).astype(BF16)
    low = low_lanes((rows, lanes), rows)
    for s in range(senders):
        hot = (
            lax.broadcasted_iota(jnp.int32, (block, lanes), 0) == rows_ref[s : s + 1, :]
        ).astype(BF16)
        one = dot(gain[jnp.minimum(slot_ref[2 * s], nodes - 1)], hot)
        two = dot(gain[jnp.minimum(slot_ref[2 * s + 1], nodes - 1)], hot)
        op[s] = jnp.where(low, one, two).astype(BF16)
    going[0].start()
    for p in range(parts):
        coming[2][p].wait()
        mine = range(p * share, (p + 1) * share)
        solved = [dot(inv[node], rhs[node]).astype(BF16) for node in mine]
        updates = [dot(below[node], value) for node, value in zip(mine, solved)]
        for i in range(0, share, 2):
            both = jnp.concatenate(updates[i : i + 2], axis=0).T.astype(BF16)
            load[:, (p * share + i) // 2] = both.reshape(levels, span, lanes)
        going[1 + p].start()
    for copy in going:
        copy.wait()


def pack(values, take_ref, level, send_ref):
    senders, span, lanes = send_ref.shape
    low = low_lanes((span, lanes), lanes // 2)
    for d in range(senders):
        first = values[take_ref[level, 2 * d]]
        second = values[take_ref[level, 2 * d + 1]]
        send_ref[d] = jnp.where(low, first, second)


def both_halves(pair_value, odd, low, half):
    turned = pltpu.roll(pair_value, half, 1)
    return jnp.where(low, turned, pair_value) if odd else jnp.where(low, pair_value, turned)


def first_kernel(take_ref, load_ref, send_ref, values):
    _, pairs, span, lanes = load_ref.shape
    low = low_lanes((span, lanes), lanes // 2)
    for pair in range(pairs):
        value = load_ref[0, pair].astype(F32)
        for odd in (0, 1):
            values[2 * pair + odd] = both_halves(value, odd, low, lanes // 2).astype(BF16)
    values[2 * pairs] = jnp.zeros((span, lanes), BF16)
    pack(values, take_ref, 0, send_ref)


def hop_kernel(
    level,
    take_ref,
    slot_ref,
    got_ref,
    all_op_ref,
    all_load_ref,
    send_ref,
    ops,
    load,
    total,
    values,
    ready,
    loaded,
):
    senders, span, lanes = got_ref.shape
    pairs = load.shape[0]
    half = lanes // 2
    parts = ready.shape[0]
    share = senders // parts
    copies = [
        pltpu.make_async_copy(
            all_op_ref.at[level, pl.ds(i * share, share)],
            ops.at[pl.ds(i * share, share)],
            ready.at[i],
        )
        for i in range(parts)
    ]
    for copy in copies:
        copy.start()
    loading = pltpu.make_async_copy(all_load_ref.at[level], load, loaded.at[0])
    loading.start()
    low = low_lanes((span, lanes), half)
    low_op = low_lanes((half, lanes), half)
    total[...] = jnp.zeros_like(total)
    for s in range(senders):
        if s == 0:
            for copy in copies[: parts // 2]:
                copy.wait()
        elif s == senders // 2:
            for copy in copies[parts // 2 :]:
                copy.wait()
        op = ops[s]
        zero = jnp.zeros_like(op)
        split = jnp.concatenate(
            [jnp.where(low_op, op, zero), jnp.where(low_op, zero, op)], axis=0
        )
        part = dot_nt(got_ref[s], split)
        one = slot_ref[level - 1, 2 * s]
        two = slot_ref[level - 1, 2 * s + 1]
        total[one] += jnp.where(low, part, 0.0)
        total[two] += jnp.where(low, 0.0, part)
    loading.wait()
    for pair in range(pairs):
        value = load[pair].astype(F32)
        for odd in (0, 1):
            node = 2 * pair + odd
            come = total[node]
            come = come + pltpu.roll(come, half, 1)
            values[node] = (both_halves(value, odd, low, half) - come).astype(BF16)
    values[2 * pairs] = jnp.zeros((span, lanes), BF16)
    pack(values, take_ref, level, send_ref)


def finish_kernel(
    early_counts,
    level_ref,
    slot_ref,
    rows_ref,
    rhs_ref,
    inv_ref,
    below_ref,
    *rest,
):
    chunks, parts = rest[-1].shape
    groups = len(early_counts)
    early = rest[:groups]
    sol_ref, out_ref, got, rhs, inv, below, inflow, base_ready, ready = rest[-9:]
    late = rest[groups:-9]
    late = [late[i : i + chunks] for i in range(0, len(late), chunks)]
    level = level_ref[0]
    step = pl.program_id(0)
    _, senders, span, lanes = got.shape
    _, nodes, block, _ = sol_ref.shape
    half = lanes // 2
    share = senders // parts
    spots = [pl.ds(p * share, share) for p in range(parts)]
    base = [
        pltpu.make_async_copy(source, target, base_ready.at[i])
        for i, (source, target) in enumerate(((rhs_ref, rhs), (inv_ref, inv), (below_ref, below)))
    ]

    @pl.when(step == 0)
    def _():
        def fetch(source):
            for p, spot in enumerate(spots):
                for c in range(chunks):
                    pltpu.make_async_copy(
                        source(c).at[spot], got.at[c, spot], ready.at[c, p]
                    ).start()

        reach = 1
        for index, (array, count) in enumerate(zip(early, early_counts)):
            inside = level < reach + count
            if index > 0:
                inside = jnp.logical_and(inside, level >= reach)

            @pl.when(inside)
            def _(array=array, reach=reach):
                fetch(lambda c: array.at[c, jnp.maximum(level - reach, 0)])

            reach += count
        for arrays in late:

            @pl.when(level == reach)
            def _(arrays=arrays):
                fetch(lambda c: arrays[c])

            reach += 1
        for copy in base:
            copy.start()

        inflow[...] = jnp.zeros_like(inflow)
        low = low_lanes((block, lanes), half)
        for s in range(senders):
            if s % share == 0:
                p = s // share
                for c in range(chunks):
                    pltpu.make_async_copy(
                        got.at[c, spots[p]], got.at[c, spots[p]], ready.at[c, p]
                    ).wait()
            hot = lax.broadcasted_iota(jnp.int32, (block, lanes), 0) == rows_ref[s : s + 1, :]
            hot = jnp.concatenate(
                [jnp.logical_and(hot, low), jnp.logical_and(hot, jnp.logical_not(low))], axis=0
            )
            part = dot(hot.astype(BF16), got[:, s].reshape(chunks * span, lanes).T)
            inflow[slot_ref[2 * s]] += part[:block]
            inflow[slot_ref[2 * s + 1]] += part[block:]
        for copy in base:
            copy.wait()

    @pl.when(step > 0)
    def _():
        at = (step - 1) * nodes
        reduced = [
            (rhs[at + n].astype(F32) - inflow[at + n]).astype(BF16) for n in range(nodes)
        ]
        solved = [dot(inv[at + n], reduced[n]).astype(BF16) for n in range(nodes)]
        for n in range(nodes):
            sol_ref[0, n] = solved[n]
        for n in range(nodes):
            out_ref[0, n] = dot(below[at + n], solved[n]).astype(BF16)


def params(limit, *semantics):
    return pltpu.CompilerParams(
        vmem_limit_bytes=limit * 1024 * 1024, dimension_semantics=semantics or None
    )


SMEM_SPEC = pl.BlockSpec(memory_space=pltpu.SMEM)
VMEM_SPEC = pl.BlockSpec(memory_space=pltpu.VMEM)
HBM_SPEC = pl.BlockSpec(memory_space=pltpu.HBM)


def shards(right_side, diag_inverse, below_block, parent_device, parent_slot, row_index):
    levels = lax.axis_size("level")
    group = lax.axis_size("grp")
    level_id = lax.axis_index("level")
    member = lax.axis_index("grp")
    _, nodes, block, columns = right_side.shape
    rows = below_block.shape[2]
    span = columns // levels
    lanes = 2 * rows
    pairs = nodes // 2
    hops = levels - 1

    devices = parent_device[:hops, :, 0].reshape(hops, group, nodes)
    slots = parent_slot[:hops].reshape(hops, group, nodes)
    place = lax.broadcasted_iota(jnp.int32, (hops, group, nodes), 2)

    def ends(named, place):
        first = jnp.min(jnp.where(named, place, nodes), axis=-1)
        last = jnp.max(jnp.where(named, place, -1), axis=-1)
        return first, jnp.where(last > first, last, nodes)

    before = jnp.maximum(level_id - 1, 0)

    def at_home(array):
        return lax.dynamic_index_in_dim(array, before, 0, keepdims=False)

    named = at_home(parent_device).reshape(group, nodes) == member
    which = jnp.where(level_id > 0, jnp.stack(ends(named, place[0])), nodes)
    hit = place[:1] == which[..., None]
    home_slot = jnp.sum(jnp.where(hit, at_home(parent_slot).reshape(group, nodes) - nodes, 0), -1)
    home_slot = (home_slot + nodes).T.reshape(-1)
    landing = at_home(row_index).reshape(rows, group, nodes) + 1
    home_rows = jnp.sum(jnp.where(hit[:, None], landing, 0), -1) - 1
    home_rows = home_rows.reshape(lanes, group).T

    parts = 4
    operators, load = pl.pallas_call(
        prepare_kernel,
        in_specs=[SMEM_SPEC, VMEM_SPEC, HBM_SPEC, HBM_SPEC, HBM_SPEC],
        out_specs=[HBM_SPEC, HBM_SPEC],
        out_shape=[
            jax.ShapeDtypeStruct((group, rows, lanes), BF16),
            jax.ShapeDtypeStruct((levels, pairs, span, lanes), BF16),
        ],
        scratch_shapes=[
            pltpu.VMEM((nodes, block, columns), BF16),
            pltpu.VMEM((nodes, block, block), BF16),
            pltpu.VMEM((nodes, rows, block), BF16),
            pltpu.VMEM((nodes, rows, block), BF16),
            pltpu.VMEM((group, rows, lanes), BF16),
            pltpu.VMEM((levels, pairs, span, lanes), BF16),
            pltpu.SemaphoreType.DMA((3, parts)),
            pltpu.SemaphoreType.DMA((1 + parts,)),
        ],
        compiler_params=params(58),
        name="prepare",
    )(home_slot, home_rows, right_side[0], diag_inverse[0], below_block[0])
    operators = lax.all_gather(operators, "level", axis=0)
    loads = lax.all_to_all(load, "level", split_axis=0, concat_axis=0, tiled=True)

    first, last = ends(devices == member, place)
    own = lax.dynamic_index_in_dim(devices, member, 1, keepdims=True)
    receiver = lax.broadcasted_iota(jnp.int32, (hops, group, nodes), 1)
    take = jnp.stack(ends(own == receiver, place), -1).reshape(hops, 2 * group)

    def slot_of(which):
        hit = place == which[..., None]
        return jnp.sum(jnp.where(hit, slots - nodes, 0), axis=-1) + nodes

    slot = jnp.stack([slot_of(first), slot_of(last)], -1).reshape(hops, 2 * group)

    message = jax.ShapeDtypeStruct((group, span, lanes), BF16)
    values_shape = pltpu.VMEM((nodes + 1, span, lanes), BF16)
    arrived = [None]
    early_counts = (hops // 2, hops - 2 - hops // 2)
    early = []
    for level in range(hops):
        if level == 0:
            send = pl.pallas_call(
                first_kernel,
                in_specs=[SMEM_SPEC, VMEM_SPEC],
                out_specs=VMEM_SPEC,
                out_shape=message,
                scratch_shapes=[values_shape],
                compiler_params=params(16),
                name="first",
            )(take, loads)
        else:
            send = pl.pallas_call(
                functools.partial(hop_kernel, level),
                in_specs=[SMEM_SPEC, SMEM_SPEC, VMEM_SPEC, HBM_SPEC, HBM_SPEC],
                out_specs=VMEM_SPEC,
                out_shape=message,
                scratch_shapes=[
                    pltpu.VMEM((group, rows, lanes), BF16),
                    pltpu.VMEM((pairs, span, lanes), BF16),
                    pltpu.VMEM((nodes + 1, span, lanes), F32),
                    values_shape,
                    pltpu.SemaphoreType.DMA((8,)),
                    pltpu.SemaphoreType.DMA((1,)),
                ],
                compiler_params=params(53),
                name="hop",
            )(take, slot, arrived[-1], operators, loads)
        arrived.append(lax.all_to_all(send, "grp", split_axis=0, concat_axis=0, tiled=True))
        if len(arrived) == 1 + sum(early_counts[: len(early) + 1]) and len(early) < 2:
            ready = jnp.stack(arrived[1 + sum(early_counts[: len(early)]) :])
            early.append(lax.all_gather(ready, "level", axis=0))
        elif len(arrived) == hops:
            arrived[-1], early[0] = lax.optimization_barrier((arrived[-1], early[0]))

    late = []
    after = lax.optimization_barrier((arrived[-2], arrived[-1]))
    for level in range(1 + sum(early_counts), levels):
        for c in range(levels):
            value = arrived[level] if c < 5 and level < hops else after[level - levels]
            late.append(value if c == level else lax.ppermute(value, "level", [(c, level)]))

    step = 16
    tail = lambda i: jnp.maximum(i - 1, 0)
    return pl.pallas_call(
        functools.partial(finish_kernel, early_counts),
        grid=(1 + nodes // step,),
        in_specs=[SMEM_SPEC, SMEM_SPEC, VMEM_SPEC]
        + [HBM_SPEC] * (3 + len(early) + len(late)),
        out_specs=[
            pl.BlockSpec((1, step, block, columns), lambda i: (0, tail(i), 0, 0)),
            pl.BlockSpec((1, step, rows, columns), lambda i: (0, tail(i), 0, 0)),
        ],
        out_shape=[
            jax.ShapeDtypeStruct((1, nodes, block, columns), BF16),
            jax.ShapeDtypeStruct((1, nodes, rows, columns), BF16),
        ],
        scratch_shapes=[
            pltpu.VMEM((levels, group, span, lanes), BF16),
            pltpu.VMEM((nodes, block, columns), BF16),
            pltpu.VMEM((nodes, block, block), BF16),
            pltpu.VMEM((nodes, rows, block), BF16),
            pltpu.VMEM((nodes + 1, block, columns), F32),
            pltpu.SemaphoreType.DMA((3,)),
            pltpu.SemaphoreType.DMA((levels, 2)),
        ],
        compiler_params=params(58, "arbitrary"),
        name="finish",
    )(
        level_id.reshape(1),
        home_slot,
        home_rows,
        right_side[0],
        diag_inverse[0],
        below_block[0],
        *early,
        *late,
    )


def solution(mesh):
    return jax.shard_map(
        shards,
        mesh=mesh,
        in_specs=(
            P("level", "grp", None, None),
            P("level", "grp", None, None),
            P("level", "grp", None, None),
            P(),
            P(),
            P(),
        ),
        out_specs=(P("level", "grp", None, None), P("level", "grp", None, None)),
        check_vma=False,
    )
```

```python
import functools

import jax
import jax.numpy as jnp
from jax import lax
from jax.experimental import pallas as pl
from jax.experimental.pallas import tpu as pltpu
from jax.sharding import PartitionSpec as P

F32 = jnp.float32
BF16 = jnp.bfloat16


def dot(a, b):
    return jnp.dot(a, b, preferred_element_type=F32)


def dot_nt(a, b):
    return lax.dot_general(a, b, (((1,), (1,)), ((), ())), preferred_element_type=F32)


def low_lanes(shape, half):
    return lax.broadcasted_iota(jnp.int32, shape, len(shape) - 1) < half


def prepare_kernel(
    slot_ref,
    rows_ref,
    rhs_ref,
    inv_ref,
    below_ref,
    op_ref,
    load_ref,
    rhs,
    inv,
    below,
    gain,
    op,
    load,
    ready,
    done,
):
    nodes, rows, block = below.shape
    levels, pairs, span, lanes = load.shape
    senders = op.shape[0]
    parts = ready.shape[1]
    share = nodes // parts
    spots = [pl.ds(p * share, share) for p in range(parts)]
    coming = [
        [
            pltpu.make_async_copy(source.at[spot], target.at[spot], ready.at[i, p])
            for p, spot in enumerate(spots)
        ]
        for i, (source, target) in enumerate(((inv_ref, inv), (below_ref, below), (rhs_ref, rhs)))
    ]
    for first, second in zip(coming[0], coming[1]):
        first.start()
        second.start()
    for copy in coming[2]:
        copy.start()
    going = [pltpu.make_async_copy(op, op_ref, done.at[0])]
    for p in range(parts):
        spot = pl.ds(p * share // 2, share // 2)
        going.append(
            pltpu.make_async_copy(load.at[:, spot], load_ref.at[:, spot], done.at[1 + p])
        )

    for p in range(parts):
        coming[0][p].wait()
        coming[1][p].wait()
        for node in range(p * share, (p + 1) * share):
            gain[node] = dot(below[node], inv[node]).astype(BF16)
    low = low_lanes((rows, lanes), rows)
    for s in range(senders):
        hot = (
            lax.broadcasted_iota(jnp.int32, (block, lanes), 0) == rows_ref[s : s + 1, :]
        ).astype(BF16)
        one = dot(gain[jnp.minimum(slot_ref[2 * s], nodes - 1)], hot)
        two = dot(gain[jnp.minimum(slot_ref[2 * s + 1], nodes - 1)], hot)
        op[s] = jnp.where(low, one, two).astype(BF16)
    going[0].start()
    for p in range(parts):
        coming[2][p].wait()
        mine = range(p * share, (p + 1) * share)
        solved = [dot(inv[node], rhs[node]).astype(BF16) for node in mine]
        updates = [dot(below[node], value) for node, value in zip(mine, solved)]
        for i in range(0, share, 2):
            both = jnp.concatenate(updates[i : i + 2], axis=0).T.astype(BF16)
            load[:, (p * share + i) // 2] = both.reshape(levels, span, lanes)
        going[1 + p].start()
    for copy in going:
        copy.wait()


def pack(values, take_ref, level, send_ref):
    senders, span, lanes = send_ref.shape
    low = low_lanes((span, lanes), lanes // 2)
    for d in range(senders):
        first = values[take_ref[level, 2 * d]]
        second = values[take_ref[level, 2 * d + 1]]
        send_ref[d] = jnp.where(low, first, second)


def both_halves(pair_value, odd, low, half):
    turned = pltpu.roll(pair_value, half, 1)
    return jnp.where(low, turned, pair_value) if odd else jnp.where(low, pair_value, turned)


def first_kernel(take_ref, load_ref, send_ref, values):
    _, pairs, span, lanes = load_ref.shape
    low = low_lanes((span, lanes), lanes // 2)
    for pair in range(pairs):
        value = load_ref[0, pair].astype(F32)
        for odd in (0, 1):
            values[2 * pair + odd] = both_halves(value, odd, low, lanes // 2).astype(BF16)
    values[2 * pairs] = jnp.zeros((span, lanes), BF16)
    pack(values, take_ref, 0, send_ref)


def hop_kernel(
    level,
    take_ref,
    slot_ref,
    got_ref,
    all_op_ref,
    all_load_ref,
    send_ref,
    ops,
    load,
    total,
    values,
    ready,
    loaded,
):
    senders, span, lanes = got_ref.shape
    pairs = load.shape[0]
    half = lanes // 2
    parts = ready.shape[0]
    share = senders // parts
    copies = [
        pltpu.make_async_copy(
            all_op_ref.at[level, pl.ds(i * share, share)],
            ops.at[pl.ds(i * share, share)],
            ready.at[i],
        )
        for i in range(parts)
    ]
    for copy in copies:
        copy.start()
    loading = pltpu.make_async_copy(all_load_ref.at[level], load, loaded.at[0])
    loading.start()
    low = low_lanes((span, lanes), half)
    low_op = low_lanes((half, lanes), half)
    total[...] = jnp.zeros_like(total)
    for s in range(senders):
        if s == 0:
            for copy in copies[: parts // 2]:
                copy.wait()
        elif s == senders // 2:
            for copy in copies[parts // 2 :]:
                copy.wait()
        op = ops[s]
        zero = jnp.zeros_like(op)
        split = jnp.concatenate(
            [jnp.where(low_op, op, zero), jnp.where(low_op, zero, op)], axis=0
        )
        part = dot_nt(got_ref[s], split)
        one = slot_ref[level - 1, 2 * s]
        two = slot_ref[level - 1, 2 * s + 1]
        total[one] += jnp.where(low, part, 0.0)
        total[two] += jnp.where(low, 0.0, part)
    loading.wait()
    for pair in range(pairs):
        value = load[pair].astype(F32)
        for odd in (0, 1):
            node = 2 * pair + odd
            come = total[node]
            come = come + pltpu.roll(come, half, 1)
            values[node] = (both_halves(value, odd, low, half) - come).astype(BF16)
    values[2 * pairs] = jnp.zeros((span, lanes), BF16)
    pack(values, take_ref, level, send_ref)


def finish_kernel(
    early_counts,
    level_ref,
    slot_ref,
    rows_ref,
    rhs_ref,
    inv_ref,
    below_ref,
    *rest,
):
    chunks, parts = rest[-1].shape
    groups = len(early_counts)
    early = rest[:groups]
    sol_ref, out_ref, got, rhs, inv, below, inflow, base_ready, ready = rest[-9:]
    late = rest[groups:-9]
    late = [late[i : i + chunks] for i in range(0, len(late), chunks)]
    level = level_ref[0]
    step = pl.program_id(0)
    _, senders, span, lanes = got.shape
    _, nodes, block, _ = sol_ref.shape
    half = lanes // 2
    share = senders // parts
    spots = [pl.ds(p * share, share) for p in range(parts)]
    base = [
        pltpu.make_async_copy(source, target, base_ready.at[i])
        for i, (source, target) in enumerate(((rhs_ref, rhs), (inv_ref, inv), (below_ref, below)))
    ]

    @pl.when(step == 0)
    def _():
        def fetch(source):
            for p, spot in enumerate(spots):
                for c in range(chunks):
                    pltpu.make_async_copy(
                        source(c).at[spot], got.at[c, spot], ready.at[c, p]
                    ).start()

        reach = 1
        for index, (array, count) in enumerate(zip(early, early_counts)):
            inside = level < reach + count
            if index > 0:
                inside = jnp.logical_and(inside, level >= reach)

            @pl.when(inside)
            def _(array=array, reach=reach):
                fetch(lambda c: array.at[c, jnp.maximum(level - reach, 0)])

            reach += count
        for arrays in late:

            @pl.when(level == reach)
            def _(arrays=arrays):
                fetch(lambda c: arrays[c])

            reach += 1
        for copy in base:
            copy.start()

        inflow[...] = jnp.zeros_like(inflow)
        low = low_lanes((block, lanes), half)
        for s in range(senders):
            if s % share == 0:
                p = s // share
                for c in range(chunks):
                    pltpu.make_async_copy(
                        got.at[c, spots[p]], got.at[c, spots[p]], ready.at[c, p]
                    ).wait()
            hot = lax.broadcasted_iota(jnp.int32, (block, lanes), 0) == rows_ref[s : s + 1, :]
            hot = jnp.concatenate(
                [jnp.logical_and(hot, low), jnp.logical_and(hot, jnp.logical_not(low))], axis=0
            )
            part = dot(hot.astype(BF16), got[:, s].reshape(chunks * span, lanes).T)
            inflow[slot_ref[2 * s]] += part[:block]
            inflow[slot_ref[2 * s + 1]] += part[block:]
        for copy in base:
            copy.wait()

    @pl.when(step > 0)
    def _():
        at = (step - 1) * nodes
        reduced = [
            (rhs[at + n].astype(F32) - inflow[at + n]).astype(BF16) for n in range(nodes)
        ]
        solved = [dot(inv[at + n], reduced[n]).astype(BF16) for n in range(nodes)]
        for n in range(nodes):
            sol_ref[0, n] = solved[n]
        for n in range(nodes):
            out_ref[0, n] = dot(below[at + n], solved[n]).astype(BF16)


def params(limit, *semantics):
    return pltpu.CompilerParams(
        vmem_limit_bytes=limit * 1024 * 1024, dimension_semantics=semantics or None
    )


SMEM_SPEC = pl.BlockSpec(memory_space=pltpu.SMEM)
VMEM_SPEC = pl.BlockSpec(memory_space=pltpu.VMEM)
HBM_SPEC = pl.BlockSpec(memory_space=pltpu.HBM)


def shards(right_side, diag_inverse, below_block, parent_device, parent_slot, row_index):
    levels = lax.axis_size("level")
    group = lax.axis_size("grp")
    level_id = lax.axis_index("level")
    member = lax.axis_index("grp")
    _, nodes, block, columns = right_side.shape
    rows = below_block.shape[2]
    span = columns // levels
    lanes = 2 * rows
    pairs = nodes // 2
    hops = levels - 1

    devices = parent_device[:hops, :, 0].reshape(hops, group, nodes)
    slots = parent_slot[:hops].reshape(hops, group, nodes)
    place = lax.broadcasted_iota(jnp.int32, (hops, group, nodes), 2)

    def ends(named, place):
        first = jnp.min(jnp.where(named, place, nodes), axis=-1)
        last = jnp.max(jnp.where(named, place, -1), axis=-1)
        return first, jnp.where(last > first, last, nodes)

    before = jnp.maximum(level_id - 1, 0)

    def at_home(array):
        return lax.dynamic_index_in_dim(array, before, 0, keepdims=False)

    named = at_home(parent_device).reshape(group, nodes) == member
    which = jnp.where(level_id > 0, jnp.stack(ends(named, place[0])), nodes)
    hit = place[:1] == which[..., None]
    home_slot = jnp.sum(jnp.where(hit, at_home(parent_slot).reshape(group, nodes) - nodes, 0), -1)
    home_slot = (home_slot + nodes).T.reshape(-1)
    landing = at_home(row_index).reshape(rows, group, nodes) + 1
    home_rows = jnp.sum(jnp.where(hit[:, None], landing, 0), -1) - 1
    home_rows = home_rows.reshape(lanes, group).T

    parts = 4
    operators, load = pl.pallas_call(
        prepare_kernel,
        in_specs=[SMEM_SPEC, VMEM_SPEC, HBM_SPEC, HBM_SPEC, HBM_SPEC],
        out_specs=[HBM_SPEC, HBM_SPEC],
        out_shape=[
            jax.ShapeDtypeStruct((group, rows, lanes), BF16),
            jax.ShapeDtypeStruct((levels, pairs, span, lanes), BF16),
        ],
        scratch_shapes=[
            pltpu.VMEM((nodes, block, columns), BF16),
            pltpu.VMEM((nodes, block, block), BF16),
            pltpu.VMEM((nodes, rows, block), BF16),
            pltpu.VMEM((nodes, rows, block), BF16),
            pltpu.VMEM((group, rows, lanes), BF16),
            pltpu.VMEM((levels, pairs, span, lanes), BF16),
            pltpu.SemaphoreType.DMA((3, parts)),
            pltpu.SemaphoreType.DMA((1 + parts,)),
        ],
        compiler_params=params(58),
        name="prepare",
    )(home_slot, home_rows, right_side[0], diag_inverse[0], below_block[0])
    operators = lax.all_gather(operators, "level", axis=0)
    loads = lax.all_to_all(load, "level", split_axis=0, concat_axis=0, tiled=True)

    first, last = ends(devices == member, place)
    own = lax.dynamic_index_in_dim(devices, member, 1, keepdims=True)
    receiver = lax.broadcasted_iota(jnp.int32, (hops, group, nodes), 1)
    take = jnp.stack(ends(own == receiver, place), -1).reshape(hops, 2 * group)

    def slot_of(which):
        hit = place == which[..., None]
        return jnp.sum(jnp.where(hit, slots - nodes, 0), axis=-1) + nodes

    slot = jnp.stack([slot_of(first), slot_of(last)], -1).reshape(hops, 2 * group)

    message = jax.ShapeDtypeStruct((group, span, lanes), BF16)
    values_shape = pltpu.VMEM((nodes + 1, span, lanes), BF16)
    arrived = [None]
    early_counts = (hops // 2, hops - 2 - hops // 2)
    early = []
    for level in range(hops):
        if level == 0:
            send = pl.pallas_call(
                first_kernel,
                in_specs=[SMEM_SPEC, VMEM_SPEC],
                out_specs=VMEM_SPEC,
                out_shape=message,
                scratch_shapes=[values_shape],
                compiler_params=params(16),
                name="first",
            )(take, loads)
        else:
            send = pl.pallas_call(
                functools.partial(hop_kernel, level),
                in_specs=[SMEM_SPEC, SMEM_SPEC, VMEM_SPEC, HBM_SPEC, HBM_SPEC],
                out_specs=VMEM_SPEC,
                out_shape=message,
                scratch_shapes=[
                    pltpu.VMEM((group, rows, lanes), BF16),
                    pltpu.VMEM((pairs, span, lanes), BF16),
                    pltpu.VMEM((nodes + 1, span, lanes), F32),
                    values_shape,
                    pltpu.SemaphoreType.DMA((8,)),
                    pltpu.SemaphoreType.DMA((1,)),
                ],
                compiler_params=params(53),
                name="hop",
            )(take, slot, arrived[-1], operators, loads)
        arrived.append(lax.all_to_all(send, "grp", split_axis=0, concat_axis=0, tiled=True))
        if len(arrived) == 1 + sum(early_counts[: len(early) + 1]) and len(early) < 2:
            ready = jnp.stack(arrived[1 + sum(early_counts[: len(early)]) :])
            early.append(lax.all_gather(ready, "level", axis=0))
        elif len(arrived) == hops:
            arrived[-1], early[0] = lax.optimization_barrier((arrived[-1], early[0]))

    sixth, seventh = arrived[-2:]
    second = levels - 2
    shared = {0: levels - 3, 1: levels - 1}
    early_sent = {
        c: lax.ppermute(sixth, "level", [(c, second)]) for c in range(levels - 3)
    }
    last_sent = {}
    for c in range(levels - 1):
        if c in shared:
            mixed = jnp.where(level_id == shared[c], sixth, seventh)
            pairs_sent = [(c, levels - 1), (shared[c], second)]
            last_sent[c] = lax.ppermute(mixed, "level", pairs_sent)
        else:
            last_sent[c] = lax.ppermute(seventh, "level", [(c, levels - 1)])
    own_sent = {second: sixth} | {source: last_sent[c] for c, source in shared.items()}
    late = [(early_sent | own_sent)[c] for c in range(levels)]
    late += [(last_sent | {levels - 1: seventh})[c] for c in range(levels)]

    step = 16
    tail = lambda i: jnp.maximum(i - 1, 0)
    return pl.pallas_call(
        functools.partial(finish_kernel, early_counts),
        grid=(1 + nodes // step,),
        in_specs=[SMEM_SPEC, SMEM_SPEC, VMEM_SPEC]
        + [HBM_SPEC] * (3 + len(early) + len(late)),
        out_specs=[
            pl.BlockSpec((1, step, block, columns), lambda i: (0, tail(i), 0, 0)),
            pl.BlockSpec((1, step, rows, columns), lambda i: (0, tail(i), 0, 0)),
        ],
        out_shape=[
            jax.ShapeDtypeStruct((1, nodes, block, columns), BF16),
            jax.ShapeDtypeStruct((1, nodes, rows, columns), BF16),
        ],
        scratch_shapes=[
            pltpu.VMEM((levels, group, span, lanes), BF16),
            pltpu.VMEM((nodes, block, columns), BF16),
            pltpu.VMEM((nodes, block, block), BF16),
            pltpu.VMEM((nodes, rows, block), BF16),
            pltpu.VMEM((nodes + 1, block, columns), F32),
            pltpu.SemaphoreType.DMA((3,)),
            pltpu.SemaphoreType.DMA((levels, 2)),
        ],
        compiler_params=params(58, "arbitrary"),
        name="finish",
    )(
        level_id.reshape(1),
        home_slot,
        home_rows,
        right_side[0],
        diag_inverse[0],
        below_block[0],
        *early,
        *late,
    )


def solution(mesh):
    return jax.shard_map(
        shards,
        mesh=mesh,
        in_specs=(
            P("level", "grp", None, None),
            P("level", "grp", None, None),
            P("level", "grp", None, None),
            P(),
            P(),
            P(),
        ),
        out_specs=(P("level", "grp", None, None), P("level", "grp", None, None)),
        check_vma=False,
    )
```
